32 devices in a mesh: dp: 4 (over y, x), expert: 8 (over z, core).
Axes of the slice: x: 2, y: 2, z: 4, core: 2. Of those that a mesh axis runs over, the one named last changes fastest.
Arguments:
- x_rows: bfloat16 [4096, 1024], P(('dp', 'expert')), may hold values from -6 to 6
- expert_ids: int32 [4096, 1], P(('dp', 'expert')), may hold values from 0 to 7; in each aligned block of 128 rows (0 to 127, 128 to 255, ...) at most 32 rows name the same one
- gates: float32 [4096, 1], P(('dp', 'expert')), may hold values from 0.1 to 1
- cotangent: bfloat16 [4096, 1024], P(('dp', 'expert')), may hold values from -6 to 6
- w_gate: bfloat16 [8, 1024, 384], P('expert', 'dp'), may hold values from -0.1875 to 0.1875
- w_up: bfloat16 [8, 1024, 384], P('expert', 'dp'), may hold values from -0.1875 to 0.1875
- w_down: bfloat16 [8, 384, 1024], P('expert', None, 'dp'), may hold values from -0.3125 to 0.3125
Outputs:
- gated_out: bfloat16 [4096, 1024], P(('dp', 'expert'))
- input_grad: bfloat16 [4096, 1024], P(('dp', 'expert'))
- gate_grad: float32 [4096, 1], P(('dp', 'expert'))
- grad_gate: bfloat16 [8, 1024, 384], P('expert', 'dp')
- grad_up: bfloat16 [8, 1024, 384], P('expert', 'dp')
- grad_down: bfloat16 [8, 384, 1024], P('expert', None, 'dp')
The draws below stay inside these ranges and needn't reach their ends.
Inputs may be any that keep to these rules, and one draw needn't show every extreme that they name: `expert_ids`: among the rows of one device each expert id occurs at most 32 times, and in some device's rows some expert occurs exactly 32 times.
All inputs are finite; a program needn't handle non-finite values.
Results may differ from the reference program's by a relative error of at most 0.009.
Values may be sent and summed in bfloat16 or wider, within the bound.
A program may use at most 64 MiB of HBM per device.

```python
import math
import jax
import jax.numpy as jnp
import numpy as np
from jax import lax

D = 1024
HID = 384
ROWS_DEV = 128
EXPERTS = 8
CAP = 32
ROWS = 4096
N_DP = 4
N_EXPERT = 8


def steps_of(stream_key, dims, cuts, smallest, high):
    factor_of, own = 1.0, jax.random.fold_in(stream_key, 6)
    for dim, parts in cuts:
        heights = jnp.exp(jax.random.uniform(jax.random.fold_in(own, dim), (parts,), jnp.float32, smallest / len(cuts), high / len(cuts)))
        factor_of = factor_of * jnp.repeat(heights, dims[dim] // parts).reshape([-1 if axis == dim else 1 for axis in range(len(dims))])
    return factor_of


def assign_block(key, own, number, rows, count, top, most, slope):
    order = jax.random.permutation(key, count)
    crowded, common = shares(count, rows * top, most, slope, True), shares(count, rows * top, most, slope, False)
    places = jnp.arange(count)

    def named(lengths, turn):
        used = int((lengths > 0).sum())
        fixed = max(1, used // 4)
        shifted = fixed + (places - fixed + turn * (used - fixed)) % max(1, count - fixed)
        return jnp.zeros((count,), jnp.int32).at[order[jnp.where(places < fixed, places, shifted)]].set(jnp.asarray(lengths, jnp.int32))

    lengths = jnp.where(number % 4 == 0, named(crowded, number // 4), named(common, number - number // 4 - 1))
    mixed = jax.random.permutation(jax.random.fold_in(own, 3), count)
    donor, receiver = mixed[0:count // 2 * 2:2], mixed[1:count // 2 * 2:2]
    room = jnp.minimum(lengths[donor] - 1, most - lengths[receiver]) // 2
    room = jnp.where((donor == order[0]) | (receiver == order[0]) | (lengths[receiver] == 0), 0, jnp.maximum(room, 0))
    shifted = jax.random.randint(jax.random.fold_in(own, 4), (count // 2,), 0, 1 << 20) % (room + 1)
    lengths = lengths.at[donor].add(-shifted).at[receiver].add(shifted)
    items = jnp.searchsorted(jnp.cumsum(lengths), jnp.arange(rows * top), side="right").astype(jnp.int32)
    listing = items.reshape(top, rows).T
    listing = listing[jax.random.permutation(jax.random.fold_in(own, 1), rows)]
    turn = jax.random.randint(jax.random.fold_in(own, 2), (rows, 1), 0, top)
    return jnp.take_along_axis(listing, (jnp.arange(top)[None, :] + turn) % top, axis=1)


def shares(amount, total, most, slope, full):
    loads = [(1 << 20) // math.isqrt(standing ** slope) + 1 for standing in range(1, amount + 1)]
    largest = most if full else min(most, max(-(-total // amount), total * loads[0] // sum(loads)))
    least = 1 if total - largest >= amount - 1 else 0
    holding, rest = [largest] + [least] * (amount - 1), total - largest - least * (amount - 1)
    while rest > 0:
        candidates = [i for i in range(1, amount) if holding[i] < largest] or [i for i in range(1, amount) if holding[i] < most]
        pool, budget = sum([loads[i] for i in candidates]), rest
        for i in candidates:
            more = min(most - holding[i], max(1, budget * loads[i] // pool), rest)
            holding[i] = holding[i] + more
            rest = rest - more
    return np.array(holding)


def scatter_about(stream_key, extent, spread, bound, split=(), kind=jnp.bfloat16):
    factor_of = steps_of(stream_key, extent, split, -0.22, 0.18) if split else 1.0
    values = jax.random.normal(stream_key, extent, jnp.float32) * spread * factor_of
    return jnp.minimum(jnp.maximum(values, -bound), bound).astype(kind)


def setup_inputs(seed: int = 0) -> dict:
    streams_of = jax.random.split(jax.random.key(seed), 8)
    x_rows = scatter_about(streams_of[0], (ROWS, D), 1.0, 6.0, ((0, 32),))
    expert_ids_keys = jax.random.split(jax.random.fold_in(streams_of[1], 1), ROWS // ROWS_DEV)
    expert_ids_turns = jax.random.permutation(jax.random.fold_in(streams_of[1], 3), ROWS // ROWS_DEV)
    expert_ids = jax.vmap(lambda own, number: assign_block(jax.random.fold_in(streams_of[1], 2), own, number, ROWS_DEV, EXPERTS, 1, CAP, 2))(expert_ids_keys, expert_ids_turns).reshape((ROWS, 1))
    gates = jnp.clip(jnp.exp(math.log(1.0) - 2.3025851 * jax.random.uniform(streams_of[2], (ROWS, 1), jnp.float32) ** steps_of(streams_of[2], (ROWS, 1), ((0, 32),), -0.2, 0.2)), 0.1, 1.0)
    cotangent = scatter_about(streams_of[3], (ROWS, D), 1.0, 6.0, ((0, 32),))
    w_gate = scatter_about(streams_of[4], (EXPERTS, D, HID), D ** -0.5, 0.1875, ((0, 8), (1, 4)))
    w_up = scatter_about(streams_of[5], (EXPERTS, D, HID), D ** -0.5, 0.1875, ((0, 8), (1, 4)))
    w_down = scatter_about(streams_of[6], (EXPERTS, HID, D), HID ** -0.5, 0.3125, ((0, 8), (2, 4)))
    return {"x_rows": x_rows, "expert_ids": expert_ids, "gates": gates, "cotangent": cotangent, "w_gate": w_gate, "w_up": w_up, "w_down": w_down}


def expert_rows(rows_in, rows_scaled, proj_gate, proj_up, proj_down):
    gate_act = jnp.dot(rows_in, proj_gate, preferred_element_type=jnp.float32)
    up_act = jnp.dot(rows_in, proj_up, preferred_element_type=jnp.float32)
    sigma = jax.nn.sigmoid(gate_act)
    hidden = (gate_act * sigma * up_act).astype(jnp.bfloat16)
    result = jnp.dot(hidden, proj_down, preferred_element_type=jnp.float32).astype(jnp.bfloat16)
    backed = jnp.dot(rows_scaled, proj_down.T, preferred_element_type=jnp.float32)
    d_gate_act = (backed * up_act * sigma * (1.0 + gate_act * (1.0 - sigma))).astype(jnp.bfloat16)
    d_up_act = (backed * gate_act * sigma).astype(jnp.bfloat16)
    d_input = (jnp.dot(d_gate_act, proj_gate.T, preferred_element_type=jnp.float32)
               + jnp.dot(d_up_act, proj_up.T, preferred_element_type=jnp.float32)).astype(jnp.bfloat16)
    grad_g = jnp.dot(rows_in.T, d_gate_act, preferred_element_type=jnp.float32)
    grad_u = jnp.dot(rows_in.T, d_up_act, preferred_element_type=jnp.float32)
    grad_d = jnp.dot(hidden.T, rows_scaled, preferred_element_type=jnp.float32)
    return result, d_input, (grad_g, grad_u, grad_d)


def group_pass(rows_in, rows_scaled, row_ids, w_gate, w_up, w_down):
    total = rows_in.shape[0]
    width = rows_in.shape[1]
    expert_count = w_gate.shape[0]
    onehot = (row_ids[:, None] == jnp.arange(expert_count, dtype=jnp.int32)[None, :]).astype(jnp.int32)
    counts = jnp.sum(onehot, 0)
    block_num = (counts + 127) // 128
    block_end = jnp.cumsum(block_num) * 128
    block_start = block_end - block_num * 128
    row_start = jnp.cumsum(counts) - counts
    order = jnp.argsort(row_ids, stable=True).astype(jnp.int32)
    sorted_ids = row_ids[order]
    target = (block_start[sorted_ids] + jnp.arange(total, dtype=jnp.int32) - row_start[sorted_ids]).astype(jnp.int32)
    padded = total + expert_count * 128
    nblocks = padded // 128
    source = jnp.full((padded,), total, jnp.int32).at[target].set(order)
    starts = jnp.arange(nblocks, dtype=jnp.int32) * 128
    block_expert = jnp.minimum(jnp.sum((block_end[None, :] <= starts[:, None]).astype(jnp.int32), 1), expert_count - 1).astype(jnp.int32)
    x_pad = jnp.concatenate([rows_in, jnp.zeros((1, width), rows_in.dtype)], 0)
    s_pad = jnp.concatenate([rows_scaled, jnp.zeros((1, width), rows_scaled.dtype)], 0)

    def advance(carry, item):
        block_rows, which = item
        result, d_input, grads = expert_rows(x_pad[block_rows], s_pad[block_rows], w_gate[which], w_up[which], w_down[which])
        carry = (carry[0].at[which].add(grads[0]), carry[1].at[which].add(grads[1]), carry[2].at[which].add(grads[2]))
        return carry, (result, d_input)

    hidden_units = w_gate.shape[2]
    init = (jnp.zeros((expert_count, width, hidden_units), jnp.float32),
            jnp.zeros((expert_count, width, hidden_units), jnp.float32),
            jnp.zeros((expert_count, hidden_units, width), jnp.float32))
    grads, (results, d_inputs) = lax.scan(advance, init, (source.reshape(nblocks, 128), block_expert))
    position = jnp.zeros((total,), jnp.int32).at[order].set(target)
    return results.reshape(padded, width)[position], d_inputs.reshape(padded, width)[position], grads


def reference(x_rows, expert_ids, gates, cotangent, w_gate, w_up, w_down):
    per_group = N_EXPERT * ROWS_DEV
    row_ids = expert_ids[:, 0].astype(jnp.int32)
    scaled = (gates * cotangent.astype(jnp.float32)).astype(jnp.bfloat16)
    results = []
    d_inputs = []
    summed = None
    for group in range(N_DP):
        lower = group * per_group
        upper = lower + per_group
        result, d_input, grads = group_pass(x_rows[lower:upper], scaled[lower:upper], row_ids[lower:upper], w_gate, w_up, w_down)
        results.append(result)
        d_inputs.append(d_input)
        rounded = lax.optimization_barrier(tuple(g.astype(jnp.bfloat16) for g in grads))
        rounded = tuple(g.astype(jnp.float32) for g in rounded)
        summed = rounded if summed is None else tuple(a + b for a, b in zip(summed, rounded))
    expert_out = jnp.concatenate(results, 0)
    input_grad = jnp.concatenate(d_inputs, 0)
    gated_out = (gates * expert_out.astype(jnp.float32)).astype(jnp.bfloat16)
    gate_grad = jnp.sum(cotangent.astype(jnp.float32) * expert_out.astype(jnp.float32), 1, keepdims=True)
    return (gated_out, input_grad, gate_grad, summed[0].astype(jnp.bfloat16),
            summed[1].astype(jnp.bfloat16), summed[2].astype(jnp.bfloat16))
```

```python
import functools

import jax
import jax.numpy as jnp
from jax import lax
from jax.experimental import pallas as pl
from jax.experimental.pallas import tpu as pltpu
from jax.sharding import PartitionSpec as P


def expert_rows(rows_in, rows_scaled, proj_gate, proj_up, proj_down):
    gate_act = jnp.dot(rows_in, proj_gate, preferred_element_type=jnp.float32)
    up_act = jnp.dot(rows_in, proj_up, preferred_element_type=jnp.float32)
    sigma = jax.nn.sigmoid(gate_act)
    hidden = (gate_act * sigma * up_act).astype(jnp.bfloat16)
    result = jnp.dot(hidden, proj_down, preferred_element_type=jnp.float32).astype(jnp.bfloat16)
    backed = jnp.dot(rows_scaled, proj_down.T, preferred_element_type=jnp.float32)
    d_gate_act = (backed * up_act * sigma * (1.0 + gate_act * (1.0 - sigma))).astype(jnp.bfloat16)
    d_up_act = (backed * gate_act * sigma).astype(jnp.bfloat16)
    d_input = (
        jnp.dot(d_gate_act, proj_gate.T, preferred_element_type=jnp.float32)
        + jnp.dot(d_up_act, proj_up.T, preferred_element_type=jnp.float32)
    ).astype(jnp.bfloat16)
    grad_g = jnp.dot(rows_in.T, d_gate_act, preferred_element_type=jnp.float32)
    grad_u = jnp.dot(rows_in.T, d_up_act, preferred_element_type=jnp.float32)
    grad_d = jnp.dot(hidden.T, rows_scaled, preferred_element_type=jnp.float32)
    return (result, d_input, (grad_g, grad_u, grad_d), (hidden, d_gate_act, d_up_act))


def rounded_sum(total, term):
    kept = lax.optimization_barrier(term.astype(jnp.bfloat16))
    return total + kept.astype(jnp.float32)


def collective_device(x_rows, expert_ids, gates, cotangent, w_gate, w_up, w_down):
    full_gate, full_up, full_down = (
        lax.all_gather(w_gate, "dp", axis=1, tiled=True),
        lax.all_gather(w_up, "dp", axis=1, tiled=True),
        lax.all_gather(w_down, "dp", axis=2, tiled=True),
    )
    proj_gate = full_gate[0]
    proj_up = full_up[0]
    proj_down = full_down[0]
    experts = lax.axis_size("expert")
    row_count = x_rows.shape[0]
    width = x_rows.shape[1]
    capacity = 2 * row_count // experts
    row_ids = expert_ids[:, 0]
    onehot = (row_ids[:, None] == jnp.arange(experts, dtype=jnp.int32)[None, :]).astype(jnp.int32)
    ranking = jnp.sum((jnp.cumsum(onehot, 0) - onehot) * onehot, 1)
    slot = row_ids * capacity + ranking
    counts = jnp.sum(onehot, 0)
    scaled = (gates * cotangent.astype(jnp.float32)).astype(jnp.bfloat16)
    send_in = (
        jnp.zeros((experts * capacity, width), jnp.bfloat16)
        .at[slot]
        .set(x_rows)
        .reshape(experts, capacity, width)
    )
    send_scaled = (
        jnp.zeros((experts * capacity, width), jnp.bfloat16)
        .at[slot]
        .set(scaled)
        .reshape(experts, capacity, width)
    )
    recv_in, recv_scaled, recv_counts = (
        lax.all_to_all(send_in, "expert", split_axis=0, concat_axis=0, tiled=True),
        lax.all_to_all(send_scaled, "expert", split_axis=0, concat_axis=0, tiled=True),
        lax.all_to_all(
            counts.reshape(experts, 1), "expert", split_axis=0, concat_axis=0, tiled=True
        ),
    )
    flat_in = recv_in.reshape(experts * capacity, width)
    flat_scaled = recv_scaled.reshape(experts * capacity, width)
    slot_out, slot_grad, grads, acts = expert_rows(
        flat_in, flat_scaled, proj_gate, proj_up, proj_down
    )
    back_result, back_input = (
        lax.all_to_all(
            slot_out.reshape(experts, capacity, width),
            "expert",
            split_axis=0,
            concat_axis=0,
            tiled=True,
        ),
        lax.all_to_all(
            slot_grad.reshape(experts, capacity, width),
            "expert",
            split_axis=0,
            concat_axis=0,
            tiled=True,
        ),
    )
    row_out = back_result.reshape(experts * capacity, width)[slot]
    input_grad = back_input.reshape(experts * capacity, width)[slot]
    gated_out = (gates * row_out.astype(jnp.float32)).astype(jnp.bfloat16)
    gate_grad = jnp.sum(
        cotangent.astype(jnp.float32) * row_out.astype(jnp.float32), 1, keepdims=True
    )
    groups = lax.axis_size("dp")
    rows_here = flat_in.shape[0]
    slice_in, slice_scaled = (
        lax.all_to_all(flat_in, "dp", split_axis=1, concat_axis=0, tiled=True),
        lax.all_to_all(flat_scaled, "dp", split_axis=1, concat_axis=0, tiled=True),
    )
    all_hidden, all_dgate, all_dup = (
        lax.all_gather(acts[0], "dp", axis=0, tiled=True),
        lax.all_gather(acts[1], "dp", axis=0, tiled=True),
        lax.all_gather(acts[2], "dp", axis=0, tiled=True),
    )
    quarter = slice_in.shape[1]
    hidden_units = all_hidden.shape[1]
    total_gate = jnp.zeros((quarter, hidden_units), jnp.float32)
    total_up = jnp.zeros((quarter, hidden_units), jnp.float32)
    total_down = jnp.zeros((hidden_units, quarter), jnp.float32)
    for group in range(groups):
        first_row = group * rows_here
        group_in = slice_in[first_row : first_row + rows_here]
        group_scaled = slice_scaled[first_row : first_row + rows_here]
        group_hidden = all_hidden[first_row : first_row + rows_here]
        group_dgate = all_dgate[first_row : first_row + rows_here]
        group_dup = all_dup[first_row : first_row + rows_here]
        total_gate = rounded_sum(
            total_gate, jnp.dot(group_in.T, group_dgate, preferred_element_type=jnp.float32)
        )
        total_up = rounded_sum(
            total_up, jnp.dot(group_in.T, group_dup, preferred_element_type=jnp.float32)
        )
        total_down = rounded_sum(
            total_down, jnp.dot(group_hidden.T, group_scaled, preferred_element_type=jnp.float32)
        )
    summed_gate = total_gate[None]
    summed_up = total_up[None]
    summed_down = total_down[None]
    return (
        gated_out,
        input_grad,
        gate_grad,
        summed_gate.astype(jnp.bfloat16),
        summed_up.astype(jnp.bfloat16),
        summed_down.astype(jnp.bfloat16),
    )


F32 = jnp.float32
BF16 = jnp.bfloat16


def dot(a, b):
    return lax.dot_general(a, b, (((1,), (0,)), ((), ())), preferred_element_type=F32)


def dot_left_t(a, b):
    return lax.dot_general(a, b, (((0,), (0,)), ((), ())), preferred_element_type=F32)


def dot_right_t(a, b):
    return lax.dot_general(a, b, (((1,), (1,)), ((), ())), preferred_element_type=F32)


def flipped(index, bits, size):
    result, place = 0, 1
    while place < size:
        digit = (index // place) % 2
        result = result + ((digit + 1) % 2 if bits & place else digit) * place
        place *= 2
    return result


def layer_kernel(
    n_dp, n_ex, cap,
    x_ref, ids_ref, gates_ref, cot_ref, wg_ref, wu_ref, wd_ref,
    gated_ref, igrad_ref, ggrad_ref, ogg_ref, ogu_ref, ogd_ref,
    place_ref, send_x, send_s, recv_x, recv_s, out_send, in_send, out_back, in_back,
    full_g, full_u, full_d, hid_ref, fac_g, fac_u, dg_ref, du_ref,
    part_g, part_u, part_d, got_g, got_u, got_d,
    z_send, z_recv, w_send, w_recv, g_send, g_recv,
):
    me_e, me_d = lax.axis_index("expert"), lax.axis_index("dp")
    z_peers = [(k, flipped(me_e, k, n_ex)) for k in range(n_ex - 1, 0, -1)]
    d_peers = [(k, flipped(me_d, k, n_dp)) for k in range(n_dp - 1, 0, -1)]
    width = x_ref.shape[1]
    piece = width // n_dp

    barrier = pltpu.get_barrier_semaphore()
    for _, peer in z_peers:
        pl.semaphore_signal(barrier, inc=1, device_id={"expert": peer}, device_id_type=pl.DeviceIdType.MESH)
    for _, peer in d_peers:
        pl.semaphore_signal(barrier, inc=1, device_id={"dp": peer}, device_id_type=pl.DeviceIdType.MESH)

    def slots(index):
        return pl.ds(pl.multiple_of(index * cap, cap), cap)

    def columns(q):
        return slice(q * piece, (q + 1) * piece)

    rows = x_ref.shape[0]
    onehot = (ids_ref[...] == lax.broadcasted_iota(jnp.int32, (rows, n_ex), 1)).astype(F32)
    earlier = (
        lax.broadcasted_iota(jnp.int32, (rows, rows), 0) > lax.broadcasted_iota(jnp.int32, (rows, rows), 1)
    ).astype(BF16)
    ranks = jnp.sum(dot(earlier, onehot.astype(BF16)) * onehot, 1, keepdims=True)
    slot = ids_ref[...] * cap + ranks.astype(jnp.int32)
    place_ref[...] = (slot == lax.broadcasted_iota(jnp.int32, (rows, n_ex * cap), 1)).astype(BF16)
    send_x[...] = dot_left_t(place_ref[...], x_ref[...]).astype(BF16)

    pl.semaphore_wait(barrier, n_dp + n_ex - 2)

    copies = []

    def z_start(which, source, target):
        made = []
        for k, peer in z_peers:
            copy = pltpu.make_async_remote_copy(
                src_ref=source.at[slots(peer)],
                dst_ref=target.at[slots(me_e)],
                send_sem=z_send.at[which, k],
                recv_sem=z_recv.at[which, k],
                device_id={"expert": peer},
                device_id_type=pl.DeviceIdType.MESH,
            )
            copy.start()
            made.append(copy)
        copies.extend(made)
        target[slots(me_e), :] = source[slots(me_e), :]
        return made

    def w_start(which, source, target):
        made = []
        for k, peer in d_peers:
            copy = pltpu.make_async_remote_copy(
                src_ref=source.at[0],
                dst_ref=target.at[me_d],
                send_sem=w_send.at[which, k],
                recv_sem=w_recv.at[which, k],
                device_id={"dp": peer},
                device_id_type=pl.DeviceIdType.MESH,
            )
            copy.start()
            made.append(copy)
        copies.extend(made)
        target[me_d] = source[0]
        return made

    def g_start(which, source, target):
        made = []
        for k, peer in d_peers:
            copy = pltpu.make_async_remote_copy(
                src_ref=source.at[peer],
                dst_ref=target.at[k],
                send_sem=g_send.at[which, k],
                recv_sem=g_recv.at[which, k],
                device_id={"dp": peer},
                device_id_type=pl.DeviceIdType.MESH,
            )
            copy.start()
            made.append(copy)
        copies.extend(made)
        return made

    def arrived(made):
        for copy in made:
            copy.wait_recv()

    x_copies = z_start(0, send_x, recv_x)
    g_copies = w_start(0, wg_ref, full_g)
    u_copies = w_start(1, wu_ref, full_u)
    d_copies = w_start(2, wd_ref, full_d)

    scaled = (gates_ref[...] * cot_ref[...].astype(F32)).astype(BF16)
    send_s[...] = dot_left_t(place_ref[...], scaled).astype(BF16)
    s_copies = z_start(1, send_s, recv_s)

    arrived(x_copies)
    arrived(g_copies)
    hidden_units = wg_ref.shape[2]
    gate_act = dot(recv_x[...], full_g[...].reshape(width, hidden_units))
    arrived(u_copies)
    up_act = dot(recv_x[...], full_u[...].reshape(width, hidden_units))
    sigma = jax.nn.sigmoid(gate_act)
    hid_ref[...] = (gate_act * sigma * up_act).astype(BF16)
    fac_g[...] = up_act * sigma * (1.0 + gate_act * (1.0 - sigma))
    fac_u[...] = gate_act * sigma
    arrived(d_copies)
    for q in range(n_dp):
        out_send[:, columns(q)] = dot(hid_ref[...], full_d[q]).astype(BF16)
    out_copies = z_start(2, out_send, out_back)

    arrived(s_copies)
    for q in range(n_dp):
        part_d[q] = dot_left_t(hid_ref[...], recv_s[:, columns(q)]).astype(BF16)
    pd_copies = g_start(2, part_d, got_d)
    backed = dot_right_t(recv_s[:, columns(0)], full_d[0])
    for q in range(1, n_dp):
        backed = backed + dot_right_t(recv_s[:, columns(q)], full_d[q])
    dg_ref[...] = (backed * fac_g[...]).astype(BF16)
    du_ref[...] = (backed * fac_u[...]).astype(BF16)
    for q in range(n_dp):
        part_g[q] = dot_left_t(recv_x[:, columns(q)], dg_ref[...]).astype(BF16)
    pg_copies = g_start(0, part_g, got_g)
    for q in range(n_dp):
        part_u[q] = dot_left_t(recv_x[:, columns(q)], du_ref[...]).astype(BF16)
    pu_copies = g_start(1, part_u, got_u)
    for q in range(n_dp):
        in_send[:, columns(q)] = (
            dot_right_t(dg_ref[...], full_g[q]) + dot_right_t(du_ref[...], full_u[q])
        ).astype(BF16)
    in_copies = z_start(3, in_send, in_back)

    arrived(out_copies)
    row_out = dot(place_ref[...], out_back[...])
    gated_ref[...] = (gates_ref[...] * row_out).astype(BF16)
    ggrad_ref[...] = jnp.sum(cot_ref[...].astype(F32) * row_out, 1, keepdims=True)
    for made, part, got, out in (
        (pd_copies, part_d, got_d, ogd_ref),
        (pg_copies, part_g, got_g, ogg_ref),
        (pu_copies, part_u, got_u, ogu_ref),
    ):
        arrived(made)
        total = part[me_d].astype(F32)
        for k in range(1, n_dp):
            total = total + got[k].astype(F32)
        out[0] = total.astype(BF16)
    arrived(in_copies)
    igrad_ref[...] = dot(place_ref[...], in_back[...]).astype(BF16)
    for copy in copies:
        copy.wait_send()


def power_of_two(size):
    return size & (size - 1) == 0


def per_device(x_rows, expert_ids, gates, cotangent, w_gate, w_up, w_down):
    n_dp, n_ex = lax.axis_size("dp"), lax.axis_size("expert")
    rows, width = x_rows.shape
    cap = 2 * rows // n_ex
    _, piece, hidden = w_gate.shape
    if cap % 16 or not power_of_two(n_ex) or not power_of_two(n_dp):
        return collective_device(x_rows, expert_ids, gates, cotangent, w_gate, w_up, w_down)
    total = n_ex * cap
    vmem = pl.BlockSpec(memory_space=pltpu.VMEM)
    slots_of = pltpu.VMEM((total, width), BF16)
    gates_of = pltpu.VMEM((n_dp, piece, hidden), BF16)
    downs_of = pltpu.VMEM((n_dp, hidden, piece), BF16)
    acts_of = pltpu.VMEM((total, hidden), BF16)
    facs_of = pltpu.VMEM((total, hidden), F32)
    return pl.pallas_call(
        functools.partial(layer_kernel, n_dp, n_ex, cap),
        out_shape=(
            jax.ShapeDtypeStruct((rows, width), BF16),
            jax.ShapeDtypeStruct((rows, width), BF16),
            jax.ShapeDtypeStruct((rows, 1), F32),
            jax.ShapeDtypeStruct(w_gate.shape, BF16),
            jax.ShapeDtypeStruct(w_up.shape, BF16),
            jax.ShapeDtypeStruct(w_down.shape, BF16),
        ),
        in_specs=[vmem] * 7,
        out_specs=[vmem] * 6,
        scratch_shapes=[
            pltpu.VMEM((rows, total), BF16),
            slots_of, slots_of, slots_of, slots_of, slots_of, slots_of, slots_of, slots_of,
            gates_of, gates_of, downs_of,
            acts_of, facs_of, facs_of, acts_of, acts_of,
            gates_of, gates_of, downs_of, gates_of, gates_of, downs_of,
            pltpu.SemaphoreType.DMA((4, n_ex)), pltpu.SemaphoreType.DMA((4, n_ex)),
            pltpu.SemaphoreType.DMA((3, n_dp)), pltpu.SemaphoreType.DMA((3, n_dp)),
            pltpu.SemaphoreType.DMA((3, n_dp)), pltpu.SemaphoreType.DMA((3, n_dp)),
        ],
        compiler_params=pltpu.CompilerParams(
            collective_id=0, has_side_effects=True, vmem_limit_bytes=40 * 1024 * 1024
        ),
    )(x_rows, expert_ids, gates, cotangent, w_gate, w_up, w_down)


def solution(mesh):
    in_specs = (
        P(("dp", "expert"), None),
        P(("dp", "expert"), None),
        P(("dp", "expert"), None),
        P(("dp", "expert"), None),
        P("expert", "dp", None),
        P("expert", "dp", None),
        P("expert", None, "dp"),
    )
    out_specs = (
        P(("dp", "expert"), None),
        P(("dp", "expert"), None),
        P(("dp", "expert"), None),
        P("expert", "dp", None),
        P("expert", "dp", None),
        P("expert", None, "dp"),
    )
    return jax.shard_map(
        per_device, mesh=mesh, in_specs=in_specs, out_specs=out_specs, check_vma=False
    )
```

```python
import functools

import jax
import jax.numpy as jnp
from jax import lax
from jax.experimental import pallas as pl
from jax.experimental.pallas import tpu as pltpu
from jax.sharding import PartitionSpec as P


def expert_rows(rows_in, rows_scaled, proj_gate, proj_up, proj_down):
    gate_act = jnp.dot(rows_in, proj_gate, preferred_element_type=jnp.float32)
    up_act = jnp.dot(rows_in, proj_up, preferred_element_type=jnp.float32)
    sigma = jax.nn.sigmoid(gate_act)
    hidden = (gate_act * sigma * up_act).astype(jnp.bfloat16)
    result = jnp.dot(hidden, proj_down, preferred_element_type=jnp.float32).astype(jnp.bfloat16)
    backed = jnp.dot(rows_scaled, proj_down.T, preferred_element_type=jnp.float32)
    d_gate_act = (backed * up_act * sigma * (1.0 + gate_act * (1.0 - sigma))).astype(jnp.bfloat16)
    d_up_act = (backed * gate_act * sigma).astype(jnp.bfloat16)
    d_input = (
        jnp.dot(d_gate_act, proj_gate.T, preferred_element_type=jnp.float32)
        + jnp.dot(d_up_act, proj_up.T, preferred_element_type=jnp.float32)
    ).astype(jnp.bfloat16)
    grad_g = jnp.dot(rows_in.T, d_gate_act, preferred_element_type=jnp.float32)
    grad_u = jnp.dot(rows_in.T, d_up_act, preferred_element_type=jnp.float32)
    grad_d = jnp.dot(hidden.T, rows_scaled, preferred_element_type=jnp.float32)
    return (result, d_input, (grad_g, grad_u, grad_d), (hidden, d_gate_act, d_up_act))


def rounded_sum(total, term):
    kept = lax.optimization_barrier(term.astype(jnp.bfloat16))
    return total + kept.astype(jnp.float32)


def collective_device(x_rows, expert_ids, gates, cotangent, w_gate, w_up, w_down):
    full_gate, full_up, full_down = (
        lax.all_gather(w_gate, "dp", axis=1, tiled=True),
        lax.all_gather(w_up, "dp", axis=1, tiled=True),
        lax.all_gather(w_down, "dp", axis=2, tiled=True),
    )
    proj_gate = full_gate[0]
    proj_up = full_up[0]
    proj_down = full_down[0]
    experts = lax.axis_size("expert")
    row_count = x_rows.shape[0]
    width = x_rows.shape[1]
    capacity = 2 * row_count // experts
    row_ids = expert_ids[:, 0]
    onehot = (row_ids[:, None] == jnp.arange(experts, dtype=jnp.int32)[None, :]).astype(jnp.int32)
    ranking = jnp.sum((jnp.cumsum(onehot, 0) - onehot) * onehot, 1)
    slot = row_ids * capacity + ranking
    counts = jnp.sum(onehot, 0)
    scaled = (gates * cotangent.astype(jnp.float32)).astype(jnp.bfloat16)
    send_in = (
        jnp.zeros((experts * capacity, width), jnp.bfloat16)
        .at[slot]
        .set(x_rows)
        .reshape(experts, capacity, width)
    )
    send_scaled = (
        jnp.zeros((experts * capacity, width), jnp.bfloat16)
        .at[slot]
        .set(scaled)
        .reshape(experts, capacity, width)
    )
    recv_in, recv_scaled, recv_counts = (
        lax.all_to_all(send_in, "expert", split_axis=0, concat_axis=0, tiled=True),
        lax.all_to_all(send_scaled, "expert", split_axis=0, concat_axis=0, tiled=True),
        lax.all_to_all(
            counts.reshape(experts, 1), "expert", split_axis=0, concat_axis=0, tiled=True
        ),
    )
    flat_in = recv_in.reshape(experts * capacity, width)
    flat_scaled = recv_scaled.reshape(experts * capacity, width)
    slot_out, slot_grad, grads, acts = expert_rows(
        flat_in, flat_scaled, proj_gate, proj_up, proj_down
    )
    back_result, back_input = (
        lax.all_to_all(
            slot_out.reshape(experts, capacity, width),
            "expert",
            split_axis=0,
            concat_axis=0,
            tiled=True,
        ),
        lax.all_to_all(
            slot_grad.reshape(experts, capacity, width),
            "expert",
            split_axis=0,
            concat_axis=0,
            tiled=True,
        ),
    )
    row_out = back_result.reshape(experts * capacity, width)[slot]
    input_grad = back_input.reshape(experts * capacity, width)[slot]
    gated_out = (gates * row_out.astype(jnp.float32)).astype(jnp.bfloat16)
    gate_grad = jnp.sum(
        cotangent.astype(jnp.float32) * row_out.astype(jnp.float32), 1, keepdims=True
    )
    groups = lax.axis_size("dp")
    rows_here = flat_in.shape[0]
    slice_in, slice_scaled = (
        lax.all_to_all(flat_in, "dp", split_axis=1, concat_axis=0, tiled=True),
        lax.all_to_all(flat_scaled, "dp", split_axis=1, concat_axis=0, tiled=True),
    )
    all_hidden, all_dgate, all_dup = (
        lax.all_gather(acts[0], "dp", axis=0, tiled=True),
        lax.all_gather(acts[1], "dp", axis=0, tiled=True),
        lax.all_gather(acts[2], "dp", axis=0, tiled=True),
    )
    quarter = slice_in.shape[1]
    hidden_units = all_hidden.shape[1]
    total_gate = jnp.zeros((quarter, hidden_units), jnp.float32)
    total_up = jnp.zeros((quarter, hidden_units), jnp.float32)
    total_down = jnp.zeros((hidden_units, quarter), jnp.float32)
    for group in range(groups):
        first_row = group * rows_here
        group_in = slice_in[first_row : first_row + rows_here]
        group_scaled = slice_scaled[first_row : first_row + rows_here]
        group_hidden = all_hidden[first_row : first_row + rows_here]
        group_dgate = all_dgate[first_row : first_row + rows_here]
        group_dup = all_dup[first_row : first_row + rows_here]
        total_gate = rounded_sum(
            total_gate, jnp.dot(group_in.T, group_dgate, preferred_element_type=jnp.float32)
        )
        total_up = rounded_sum(
            total_up, jnp.dot(group_in.T, group_dup, preferred_element_type=jnp.float32)
        )
        total_down = rounded_sum(
            total_down, jnp.dot(group_hidden.T, group_scaled, preferred_element_type=jnp.float32)
        )
    summed_gate = total_gate[None]
    summed_up = total_up[None]
    summed_down = total_down[None]
    return (
        gated_out,
        input_grad,
        gate_grad,
        summed_gate.astype(jnp.bfloat16),
        summed_up.astype(jnp.bfloat16),
        summed_down.astype(jnp.bfloat16),
    )


F32 = jnp.float32
BF16 = jnp.bfloat16


def dot(a, b):
    return lax.dot_general(a, b, (((1,), (0,)), ((), ())), preferred_element_type=F32)


def dot_left_t(a, b):
    return lax.dot_general(a, b, (((0,), (0,)), ((), ())), preferred_element_type=F32)


def dot_right_t(a, b):
    return lax.dot_general(a, b, (((1,), (1,)), ((), ())), preferred_element_type=F32)


def flipped(index, bits, size):
    result, place = 0, 1
    while place < size:
        digit = (index // place) % 2
        result = result + ((digit + 1) % 2 if bits & place else digit) * place
        place *= 2
    return result


def layer_kernel(
    n_dp, n_ex, cap,
    x_hbm, ids_hbm, gates_hbm, cot_hbm, wg_hbm, wu_hbm, wd_hbm,
    gated_hbm, igrad_hbm, ggrad_hbm, ogg_hbm, ogu_hbm, ogd_hbm,
    gated_ref, igrad_ref, ggrad_ref, ogg_ref, ogu_ref, ogd_ref,
    x_ref, ids_ref, gates_ref, cot_ref,
    place_ref, send_x, send_s, recv_x, recv_s, out_send, in_send, out_back, in_back,
    full_g, full_u, full_d, hid_ref, fac_g, fac_u, dg_ref, du_ref,
    part_g, part_u, part_d, got_g, got_u, got_d, sum_g, sum_u, sum_d,
    own_sem, out_sem, z_send, z_recv, w_send, w_recv, g_send, g_recv,
):
    me_e, me_d = lax.axis_index("expert"), lax.axis_index("dp")
    z_peers = [(k, flipped(me_e, k, n_ex)) for k in range(n_ex - 1, 0, -1)]
    side, over, across = (flipped(me_d, k, n_dp) for k in (1, 2, 3))
    rows, width = x_ref.shape
    piece = width // n_dp

    barrier = pltpu.get_barrier_semaphore()
    for _, peer in z_peers:
        pl.semaphore_signal(barrier, inc=1, device_id={"expert": peer}, device_id_type=pl.DeviceIdType.MESH)
    for peer in (side, over):
        pl.semaphore_signal(barrier, inc=1, device_id={"dp": peer}, device_id_type=pl.DeviceIdType.MESH)

    own = []
    for source, target in (
        (ids_hbm, ids_ref), (x_hbm, x_ref), (gates_hbm, gates_ref), (cot_hbm, cot_ref),
        (wg_hbm.at[0], full_g.at[me_d]), (wu_hbm.at[0], full_u.at[me_d]), (wd_hbm.at[0], full_d.at[me_d]),
    ):
        copy = pltpu.make_async_copy(source, target, own_sem.at[len(own)])
        copy.start()
        own.append(copy)

    def columns(q):
        return slice(q * piece, (q + 1) * piece)

    copies = []

    def remote(source, target, send_sem, recv_sem, axis, peer):
        copy = pltpu.make_async_remote_copy(
            src_ref=source,
            dst_ref=target,
            send_sem=send_sem,
            recv_sem=recv_sem,
            device_id={axis: peer},
            device_id_type=pl.DeviceIdType.MESH,
        )
        copy.start()
        copies.append(copy)
        return copy

    def slots(index):
        return pl.ds(pl.multiple_of(index * cap, cap), cap)

    def z_start(which, source, target, k):
        peer = flipped(me_e, k, n_ex)
        return remote(
            source.at[slots(peer)], target.at[slots(me_e)],
            z_send.at[which, k], z_recv.at[which, k], "expert", peer,
        )

    def z_own(source, target):
        target[slots(me_e), :] = source[slots(me_e), :]

    def w_start(which, source, target):
        return [
            remote(
                source.at[0], target.at[me_d],
                w_send.at[which, k], w_recv.at[which, k], "dp", peer,
            )
            for k, peer in enumerate((side, over))
        ]

    def w_pass(which, target, direct):
        half = target.shape[1] // 2
        first, second = target.at[side, pl.ds(0, half)], target.at[over, pl.ds(half, half)]
        direct[0].wait_recv()
        one = remote(first, first, w_send.at[which, 2], w_recv.at[which, 2], "dp", over)
        direct[1].wait_recv()
        two = remote(second, second, w_send.at[which, 3], w_recv.at[which, 3], "dp", side)
        return [one, two]

    def g_start(which, part, got):
        half = part.shape[1] // 2
        upper, lower = pl.ds(0, half), pl.ds(half, half)
        made = {}
        for slot, source, peer in (
            (1, part.at[across, upper], side),
            (3, part.at[across, lower], over),
            (0, part.at[side, upper], side),
            (2, part.at[over, lower], over),
        ):
            made[slot] = remote(
                source, got.at[slot], g_send.at[which, slot], g_recv.at[which, slot], "dp", peer
            )
        return made

    def g_pass(which, part, got, total, made):
        half = part.shape[1] // 2
        for slot, peer, rows_of in ((1, over, pl.ds(0, half)), (3, side, pl.ds(half, half))):
            made[slot].wait_recv()
            index, later = slot // 2, 4 + slot // 2
            total[index] = (part[peer, rows_of].astype(F32) + got[slot].astype(F32)).astype(BF16)
            made[later] = remote(
                total.at[index], got.at[later], g_send.at[which, later], g_recv.at[which, later], "dp", peer
            )

    def g_finish(part, got, made, out):
        half = part.shape[1] // 2
        for slot, later, rows_of in ((0, 4, pl.ds(0, half)), (2, 5, pl.ds(half, half))):
            made[slot].wait_recv()
            made[later].wait_recv()
            out[0, rows_of] = (
                part[me_d, rows_of].astype(F32) + got[slot].astype(F32) + got[later].astype(F32)
            ).astype(BF16)

    stored = []

    def store(source, target):
        copy = pltpu.make_async_copy(source, target, out_sem.at[len(stored)])
        copy.start()
        stored.append(copy)

    def arrived(made):
        for copy in made:
            copy.wait_recv()

    far = [k for k in range(n_ex - 1, 0, -1) if k >= n_ex // 2]
    near = [k for k in range(n_ex - 1, 0, -1) if k < n_ex // 2]

    own[0].wait()
    ids = ids_ref[...]
    onehot = (ids == lax.broadcasted_iota(jnp.int32, (n_ex, rows), 0)).astype(F32)
    row_a = lax.broadcasted_iota(jnp.int32, (rows, rows), 0)
    row_b = lax.broadcasted_iota(jnp.int32, (rows, rows), 1)
    ranks = jnp.sum(dot(onehot.astype(BF16), (row_a < row_b).astype(BF16)) * onehot, 0, keepdims=True)
    slot = ids * cap + ranks.astype(jnp.int32)
    place_ref[...] = (slot == lax.broadcasted_iota(jnp.int32, (n_ex * cap, rows), 0)).astype(BF16)
    own[1].wait()
    send_x[...] = dot(place_ref[...], x_ref[...]).astype(BF16)

    pl.semaphore_wait(barrier, n_ex + 1)

    x_copies = [z_start(0, send_x, recv_x, k) for k in far]
    g_direct = w_start(0, wg_hbm, full_g)
    u_direct = w_start(1, wu_hbm, full_u)

    own[2].wait()
    own[3].wait()
    diagonal = row_a == row_b
    gates = jnp.sum(jnp.where(diagonal, gates_ref[...], 0.0), 1, keepdims=True)
    scaled = (gates * cot_ref[...].astype(F32)).astype(BF16)
    send_s[...] = dot(place_ref[...], scaled).astype(BF16)
    s_copies = []
    for step, k in enumerate(far):
        s_copies.append(z_start(1, send_s, recv_s, k))
        if step < len(near):
            x_copies.append(z_start(0, send_x, recv_x, near[step]))
    s_copies += [z_start(1, send_s, recv_s, k) for k in near]
    z_own(send_x, recv_x)
    z_own(send_s, recv_s)

    g_passed = w_pass(0, full_g, g_direct)
    d_direct = w_start(2, wd_hbm, full_d)
    u_passed = w_pass(1, full_u, u_direct)
    hidden_units = wg_hbm.shape[2]
    arrived(x_copies)
    arrived(g_passed)
    own[4].wait()
    gate_act = dot(recv_x[...], full_g[...].reshape(width, hidden_units))
    d_passed = w_pass(2, full_d, d_direct)
    arrived(u_passed)
    own[5].wait()
    up_act = dot(recv_x[...], full_u[...].reshape(width, hidden_units))
    sigma = jax.nn.sigmoid(gate_act)
    hid_ref[...] = (gate_act * sigma * up_act).astype(BF16)
    fac_g[...] = up_act * sigma * (1.0 + gate_act * (1.0 - sigma))
    fac_u[...] = gate_act * sigma
    arrived(d_passed)
    own[6].wait()
    for q in range(n_dp):
        out_send[:, columns(q)] = dot(hid_ref[...], full_d[q]).astype(BF16)
    out_copies = [z_start(2, out_send, out_back, k) for k in far + near]
    z_own(out_send, out_back)

    arrived(s_copies)
    for q in range(n_dp):
        part_d[q] = dot_left_t(hid_ref[...], recv_s[:, columns(q)]).astype(BF16)
    pd_copies = g_start(2, part_d, got_d)
    backed = dot_right_t(recv_s[:, columns(0)], full_d[0])
    for q in range(1, n_dp):
        backed = backed + dot_right_t(recv_s[:, columns(q)], full_d[q])
    dg_ref[...] = (backed * fac_g[...]).astype(BF16)
    du_ref[...] = (backed * fac_u[...]).astype(BF16)
    for q in range(n_dp):
        part_g[q] = dot_left_t(recv_x[:, columns(q)], dg_ref[...]).astype(BF16)
    pg_copies = g_start(0, part_g, got_g)
    for q in range(n_dp):
        part_u[q] = dot_left_t(recv_x[:, columns(q)], du_ref[...]).astype(BF16)
    pu_copies = g_start(1, part_u, got_u)
    for q in range(n_dp):
        in_send[:, columns(q)] = (
            dot_right_t(dg_ref[...], full_g[q]) + dot_right_t(du_ref[...], full_u[q])
        ).astype(BF16)
    in_copies = [z_start(3, in_send, in_back, k) for k in far + near]
    z_own(in_send, in_back)
    g_pass(2, part_d, got_d, sum_d, pd_copies)
    g_pass(0, part_g, got_g, sum_g, pg_copies)
    g_pass(1, part_u, got_u, sum_u, pu_copies)

    arrived(out_copies)
    row_out = dot_left_t(place_ref[...], out_back[...])
    gated_ref[...] = (gates * row_out).astype(BF16)
    row_sums = jnp.sum(cot_ref[...].astype(F32) * row_out, 1, keepdims=True)
    ggrad_ref[...] = jnp.sum(jnp.where(diagonal, row_sums, 0.0), 0, keepdims=True)
    store(gated_ref, gated_hbm)
    store(ggrad_ref, ggrad_hbm)
    g_finish(part_d, got_d, pd_copies, ogd_ref)
    store(ogd_ref, ogd_hbm)
    g_finish(part_g, got_g, pg_copies, ogg_ref)
    store(ogg_ref, ogg_hbm)
    g_finish(part_u, got_u, pu_copies, ogu_ref)
    store(ogu_ref, ogu_hbm)
    arrived(in_copies)
    igrad_ref[...] = dot_left_t(place_ref[...], in_back[...]).astype(BF16)
    store(igrad_ref, igrad_hbm)
    for copy in copies:
        copy.wait_send()
    for copy in stored:
        copy.wait()


def results_kernel(*refs):
    count = len(refs) // 2
    sources, targets, sem = refs[:count], refs[count:-1], refs[-1]
    made = [
        pltpu.make_async_copy(source, target, sem.at[i])
        for i, (source, target) in enumerate(zip(sources, targets))
    ]
    for copy in made:
        copy.start()
    for copy in made:
        copy.wait()


def power_of_two(size):
    return size & (size - 1) == 0


def per_device(x_rows, expert_ids, gates, cotangent, w_gate, w_up, w_down):
    n_dp, n_ex = lax.axis_size("dp"), lax.axis_size("expert")
    rows, width = x_rows.shape
    cap = 2 * rows // n_ex
    _, piece, hidden = w_gate.shape
    if cap % 16 or piece % 32 or hidden % 32 or not power_of_two(n_ex) or n_dp != 4:
        return collective_device(x_rows, expert_ids, gates, cotangent, w_gate, w_up, w_down)
    total = n_ex * cap
    hbm = pl.BlockSpec(memory_space=pltpu.HBM)
    slots_of = pltpu.VMEM((total, width), BF16)
    gates_of = pltpu.VMEM((n_dp, piece, hidden), BF16)
    downs_of = pltpu.VMEM((n_dp, hidden, piece), BF16)
    got_gates = pltpu.VMEM((6, piece // 2, hidden), BF16)
    got_downs = pltpu.VMEM((6, hidden // 2, piece), BF16)
    sum_gates = pltpu.VMEM((2, piece // 2, hidden), BF16)
    sum_downs = pltpu.VMEM((2, hidden // 2, piece), BF16)
    acts_of = pltpu.VMEM((total, hidden), BF16)
    facs_of = pltpu.VMEM((total, hidden), F32)
    shapes = (
        jax.ShapeDtypeStruct((rows, width), BF16),
        jax.ShapeDtypeStruct((rows, width), BF16),
        jax.ShapeDtypeStruct((1, rows), F32),
        jax.ShapeDtypeStruct(w_gate.shape, BF16),
        jax.ShapeDtypeStruct(w_up.shape, BF16),
        jax.ShapeDtypeStruct(w_down.shape, BF16),
    )
    results = pl.pallas_call(
        functools.partial(layer_kernel, n_dp, n_ex, cap),
        out_shape=shapes,
        in_specs=[hbm] * 7,
        out_specs=[hbm] * 6,
        scratch_shapes=[
            *(pltpu.VMEM(shape.shape, shape.dtype) for shape in shapes),
            pltpu.VMEM((rows, width), BF16), pltpu.VMEM((1, rows), jnp.int32),
            pltpu.VMEM((1, rows), F32), pltpu.VMEM((rows, width), BF16),
            pltpu.VMEM((total, rows), BF16),
            slots_of, slots_of, slots_of, slots_of, slots_of, slots_of, slots_of, slots_of,
            gates_of, gates_of, downs_of,
            acts_of, facs_of, facs_of, acts_of, acts_of,
            gates_of, gates_of, downs_of,
            got_gates, got_gates, got_downs, sum_gates, sum_gates, sum_downs,
            pltpu.SemaphoreType.DMA((7,)), pltpu.SemaphoreType.DMA((6,)),
            pltpu.SemaphoreType.DMA((4, n_ex)), pltpu.SemaphoreType.DMA((4, n_ex)),
            pltpu.SemaphoreType.DMA((3, 4)), pltpu.SemaphoreType.DMA((3, 4)),
            pltpu.SemaphoreType.DMA((3, 6)), pltpu.SemaphoreType.DMA((3, 6)),
        ],
        compiler_params=pltpu.CompilerParams(
            collective_id=0, has_side_effects=True, vmem_limit_bytes=64 * 1024 * 1024
        ),
    )(
        x_rows, expert_ids.reshape(1, rows), gates.reshape(1, rows), cotangent,
        w_gate, w_up, w_down,
    )
    results = pl.pallas_call(
        results_kernel,
        out_shape=shapes,
        in_specs=[hbm] * 6,
        out_specs=[hbm] * 6,
        scratch_shapes=[pltpu.SemaphoreType.DMA((6,))],
        compiler_params=pltpu.CompilerParams(vmem_limit_bytes=64 * 1024 * 1024),
    )(*results)
    return (*results[:2], results[2].reshape(rows, 1), *results[3:])


def solution(mesh):
    in_specs = (
        P(("dp", "expert"), None),
        P(("dp", "expert"), None),
        P(("dp", "expert"), None),
        P(("dp", "expert"), None),
        P("expert", "dp", None),
        P("expert", "dp", None),
        P("expert", None, "dp"),
    )
    out_specs = (
        P(("dp", "expert"), None),
        P(("dp", "expert"), None),
        P(("dp", "expert"), None),
        P("expert", "dp", None),
        P("expert", "dp", None),
        P("expert", None, "dp"),
    )
    return jax.shard_map(
        per_device, mesh=mesh, in_specs=in_specs, out_specs=out_specs, check_vma=False
    )
```

```python
import functools

import jax
import jax.numpy as jnp
from jax import lax
from jax.experimental import pallas as pl
from jax.experimental.pallas import tpu as pltpu
from jax.sharding import PartitionSpec as P


def expert_rows(rows_in, rows_scaled, proj_gate, proj_up, proj_down):
    gate_act = jnp.dot(rows_in, proj_gate, preferred_element_type=jnp.float32)
    up_act = jnp.dot(rows_in, proj_up, preferred_element_type=jnp.float32)
    sigma = jax.nn.sigmoid(gate_act)
    hidden = (gate_act * sigma * up_act).astype(jnp.bfloat16)
    result = jnp.dot(hidden, proj_down, preferred_element_type=jnp.float32).astype(jnp.bfloat16)
    backed = jnp.dot(rows_scaled, proj_down.T, preferred_element_type=jnp.float32)
    d_gate_act = (backed * up_act * sigma * (1.0 + gate_act * (1.0 - sigma))).astype(jnp.bfloat16)
    d_up_act = (backed * gate_act * sigma).astype(jnp.bfloat16)
    d_input = (
        jnp.dot(d_gate_act, proj_gate.T, preferred_element_type=jnp.float32)
        + jnp.dot(d_up_act, proj_up.T, preferred_element_type=jnp.float32)
    ).astype(jnp.bfloat16)
    grad_g = jnp.dot(rows_in.T, d_gate_act, preferred_element_type=jnp.float32)
    grad_u = jnp.dot(rows_in.T, d_up_act, preferred_element_type=jnp.float32)
    grad_d = jnp.dot(hidden.T, rows_scaled, preferred_element_type=jnp.float32)
    return (result, d_input, (grad_g, grad_u, grad_d), (hidden, d_gate_act, d_up_act))


def rounded_sum(total, term):
    kept = lax.optimization_barrier(term.astype(jnp.bfloat16))
    return total + kept.astype(jnp.float32)


def collective_device(x_rows, expert_ids, gates, cotangent, w_gate, w_up, w_down):
    full_gate, full_up, full_down = (
        lax.all_gather(w_gate, "dp", axis=1, tiled=True),
        lax.all_gather(w_up, "dp", axis=1, tiled=True),
        lax.all_gather(w_down, "dp", axis=2, tiled=True),
    )
    proj_gate = full_gate[0]
    proj_up = full_up[0]
    proj_down = full_down[0]
    experts = lax.axis_size("expert")
    row_count = x_rows.shape[0]
    width = x_rows.shape[1]
    capacity = 2 * row_count // experts
    row_ids = expert_ids[:, 0]
    onehot = (row_ids[:, None] == jnp.arange(experts, dtype=jnp.int32)[None, :]).astype(jnp.int32)
    ranking = jnp.sum((jnp.cumsum(onehot, 0) - onehot) * onehot, 1)
    slot = row_ids * capacity + ranking
    counts = jnp.sum(onehot, 0)
    scaled = (gates * cotangent.astype(jnp.float32)).astype(jnp.bfloat16)
    send_in = (
        jnp.zeros((experts * capacity, width), jnp.bfloat16)
        .at[slot]
        .set(x_rows)
        .reshape(experts, capacity, width)
    )
    send_scaled = (
        jnp.zeros((experts * capacity, width), jnp.bfloat16)
        .at[slot]
        .set(scaled)
        .reshape(experts, capacity, width)
    )
    recv_in, recv_scaled, recv_counts = (
        lax.all_to_all(send_in, "expert", split_axis=0, concat_axis=0, tiled=True),
        lax.all_to_all(send_scaled, "expert", split_axis=0, concat_axis=0, tiled=True),
        lax.all_to_all(
            counts.reshape(experts, 1), "expert", split_axis=0, concat_axis=0, tiled=True
        ),
    )
    flat_in = recv_in.reshape(experts * capacity, width)
    flat_scaled = recv_scaled.reshape(experts * capacity, width)
    slot_out, slot_grad, grads, acts = expert_rows(
        flat_in, flat_scaled, proj_gate, proj_up, proj_down
    )
    back_result, back_input = (
        lax.all_to_all(
            slot_out.reshape(experts, capacity, width),
            "expert",
            split_axis=0,
            concat_axis=0,
            tiled=True,
        ),
        lax.all_to_all(
            slot_grad.reshape(experts, capacity, width),
            "expert",
            split_axis=0,
            concat_axis=0,
            tiled=True,
        ),
    )
    row_out = back_result.reshape(experts * capacity, width)[slot]
    input_grad = back_input.reshape(experts * capacity, width)[slot]
    gated_out = (gates * row_out.astype(jnp.float32)).astype(jnp.bfloat16)
    gate_grad = jnp.sum(
        cotangent.astype(jnp.float32) * row_out.astype(jnp.float32), 1, keepdims=True
    )
    groups = lax.axis_size("dp")
    rows_here = flat_in.shape[0]
    slice_in, slice_scaled = (
        lax.all_to_all(flat_in, "dp", split_axis=1, concat_axis=0, tiled=True),
        lax.all_to_all(flat_scaled, "dp", split_axis=1, concat_axis=0, tiled=True),
    )
    all_hidden, all_dgate, all_dup = (
        lax.all_gather(acts[0], "dp", axis=0, tiled=True),
        lax.all_gather(acts[1], "dp", axis=0, tiled=True),
        lax.all_gather(acts[2], "dp", axis=0, tiled=True),
    )
    quarter = slice_in.shape[1]
    hidden_units = all_hidden.shape[1]
    total_gate = jnp.zeros((quarter, hidden_units), jnp.float32)
    total_up = jnp.zeros((quarter, hidden_units), jnp.float32)
    total_down = jnp.zeros((hidden_units, quarter), jnp.float32)
    for group in range(groups):
        first_row = group * rows_here
        group_in = slice_in[first_row : first_row + rows_here]
        group_scaled = slice_scaled[first_row : first_row + rows_here]
        group_hidden = all_hidden[first_row : first_row + rows_here]
        group_dgate = all_dgate[first_row : first_row + rows_here]
        group_dup = all_dup[first_row : first_row + rows_here]
        total_gate = rounded_sum(
            total_gate, jnp.dot(group_in.T, group_dgate, preferred_element_type=jnp.float32)
        )
        total_up = rounded_sum(
            total_up, jnp.dot(group_in.T, group_dup, preferred_element_type=jnp.float32)
        )
        total_down = rounded_sum(
            total_down, jnp.dot(group_hidden.T, group_scaled, preferred_element_type=jnp.float32)
        )
    summed_gate = total_gate[None]
    summed_up = total_up[None]
    summed_down = total_down[None]
    return (
        gated_out,
        input_grad,
        gate_grad,
        summed_gate.astype(jnp.bfloat16),
        summed_up.astype(jnp.bfloat16),
        summed_down.astype(jnp.bfloat16),
    )


F32 = jnp.float32
BF16 = jnp.bfloat16


def dot(a, b):
    return lax.dot_general(a, b, (((1,), (0,)), ((), ())), preferred_element_type=F32)


def dot_left_t(a, b):
    return lax.dot_general(a, b, (((0,), (0,)), ((), ())), preferred_element_type=F32)


def dot_right_t(a, b):
    return lax.dot_general(a, b, (((1,), (1,)), ((), ())), preferred_element_type=F32)


def flipped(index, bits, size):
    result, place = 0, 1
    while place < size:
        digit = (index // place) % 2
        result = result + ((digit + 1) % 2 if bits & place else digit) * place
        place *= 2
    return result


def layer_kernel(
    n_dp, n_ex, cap,
    x_hbm, ids_hbm, gates_hbm, cot_hbm, wg_hbm, wu_hbm, wd_hbm,
    gated_hbm, igrad_hbm, ggrad_hbm, ogg_hbm, ogu_hbm, ogd_hbm,
    gated_ref, igrad_ref, ggrad_ref, ogg_ref, ogu_ref, ogd_ref,
    x_ref, ids_ref, gates_ref, cot_ref,
    place_ref, send_x, send_s, recv_x, recv_s, out_send, in_send, out_back, in_back,
    full_g, full_u, full_d, hid_ref, fac_g, fac_u, dg_ref, du_ref,
    part_g, part_u, part_d, got_g, got_u, got_d, sum_g, sum_u, sum_d,
    own_sem, out_sem, z_send, z_recv, w_send, w_recv, g_send, g_recv,
):
    me_e, me_d = lax.axis_index("expert"), lax.axis_index("dp")
    z_peers = [(k, flipped(me_e, k, n_ex)) for k in range(n_ex - 1, 0, -1)]
    side, over, across = (flipped(me_d, k, n_dp) for k in (1, 2, 3))
    rows, width = x_ref.shape
    piece = width // n_dp

    barrier = pltpu.get_barrier_semaphore()
    for _, peer in z_peers:
        pl.semaphore_signal(barrier, inc=1, device_id={"expert": peer}, device_id_type=pl.DeviceIdType.MESH)
    for peer in (side, over):
        pl.semaphore_signal(barrier, inc=1, device_id={"dp": peer}, device_id_type=pl.DeviceIdType.MESH)

    own = []
    for source, target in (
        (ids_hbm, ids_ref), (x_hbm, x_ref), (gates_hbm, gates_ref), (cot_hbm, cot_ref),
        (wg_hbm.at[0], full_g.at[me_d]), (wu_hbm.at[0], full_u.at[me_d]), (wd_hbm.at[0], full_d.at[me_d]),
    ):
        copy = pltpu.make_async_copy(source, target, own_sem.at[len(own)])
        copy.start()
        own.append(copy)

    def columns(q):
        return slice(q * piece, (q + 1) * piece)

    copies = []

    def remote(source, target, send_sem, recv_sem, axis, peer):
        copy = pltpu.make_async_remote_copy(
            src_ref=source,
            dst_ref=target,
            send_sem=send_sem,
            recv_sem=recv_sem,
            device_id={axis: peer},
            device_id_type=pl.DeviceIdType.MESH,
        )
        copy.start()
        copies.append(copy)
        return copy

    def slots(index):
        return pl.ds(pl.multiple_of(index * cap, cap), cap)

    def z_start(which, source, target, k):
        peer = flipped(me_e, k, n_ex)
        return remote(
            source.at[slots(peer)], target.at[slots(me_e)],
            z_send.at[which, k], z_recv.at[which, k], "expert", peer,
        )

    def z_own(source, target):
        target[slots(me_e), :] = source[slots(me_e), :]

    def w_start(which, source, target):
        return [
            remote(
                source.at[0], target.at[me_d],
                w_send.at[which, k], w_recv.at[which, k], "dp", peer,
            )
            for k, peer in enumerate((side, over))
        ]

    def w_pass(which, target, direct):
        half = target.shape[1] // 2
        first, second = target.at[side, pl.ds(0, half)], target.at[over, pl.ds(half, half)]
        direct[0].wait_recv()
        one = remote(first, first, w_send.at[which, 2], w_recv.at[which, 2], "dp", over)
        direct[1].wait_recv()
        two = remote(second, second, w_send.at[which, 3], w_recv.at[which, 3], "dp", side)
        return [one, two]

    def g_start(which, part, got):
        half = part.shape[1] // 2
        upper, lower = pl.ds(0, half), pl.ds(half, half)
        made = {}
        for slot, source, peer in (
            (1, part.at[across, upper], side),
            (3, part.at[across, lower], over),
            (0, part.at[side, upper], side),
            (2, part.at[over, lower], over),
        ):
            made[slot] = remote(
                source, got.at[slot], g_send.at[which, slot], g_recv.at[which, slot], "dp", peer
            )
        return made

    def g_pass(which, part, got, total, made):
        half = part.shape[1] // 2
        for slot, peer, rows_of in ((1, over, pl.ds(0, half)), (3, side, pl.ds(half, half))):
            made[slot].wait_recv()
            index, later = slot // 2, 4 + slot // 2
            total[index] = (part[peer, rows_of].astype(F32) + got[slot].astype(F32)).astype(BF16)
            made[later] = remote(
                total.at[index], got.at[later], g_send.at[which, later], g_recv.at[which, later], "dp", peer
            )

    def g_finish(part, got, made, out):
        half = part.shape[1] // 2
        for slot, later, rows_of in ((0, 4, pl.ds(0, half)), (2, 5, pl.ds(half, half))):
            made[slot].wait_recv()
            made[later].wait_recv()
            out[0, rows_of] = (
                part[me_d, rows_of].astype(F32) + got[slot].astype(F32) + got[later].astype(F32)
            ).astype(BF16)

    stored = []

    def store(source, target):
        copy = pltpu.make_async_copy(source, target, out_sem.at[len(stored)])
        copy.start()
        stored.append(copy)

    def arrived(made):
        for copy in made:
            copy.wait_recv()

    far = [k for k in range(n_ex - 1, 0, -1) if k >= n_ex // 2]
    near = [k for k in range(n_ex - 1, 0, -1) if k < n_ex // 2]

    own[0].wait()
    ids = ids_ref[...]
    onehot = (ids == lax.broadcasted_iota(jnp.int32, (n_ex, rows), 0)).astype(F32)
    row_a = lax.broadcasted_iota(jnp.int32, (rows, rows), 0)
    row_b = lax.broadcasted_iota(jnp.int32, (rows, rows), 1)
    ranks = jnp.sum(dot(onehot.astype(BF16), (row_a < row_b).astype(BF16)) * onehot, 0, keepdims=True)
    slot = ids * cap + ranks.astype(jnp.int32)
    place_ref[...] = (slot == lax.broadcasted_iota(jnp.int32, (n_ex * cap, rows), 0)).astype(BF16)
    own[1].wait()
    send_x[...] = dot(place_ref[...], x_ref[...]).astype(BF16)

    pl.semaphore_wait(barrier, n_ex + 1)

    x_copies = [z_start(0, send_x, recv_x, k) for k in far]
    g_direct = w_start(0, wg_hbm, full_g)
    u_direct = w_start(1, wu_hbm, full_u)

    own[2].wait()
    own[3].wait()
    diagonal = row_a == row_b
    gates = jnp.sum(jnp.where(diagonal, gates_ref[...], 0.0), 1, keepdims=True)
    scaled = (gates * cot_ref[...].astype(F32)).astype(BF16)
    send_s[...] = dot(place_ref[...], scaled).astype(BF16)
    s_copies = []
    for step, k in enumerate(far):
        s_copies.append(z_start(1, send_s, recv_s, k))
        if step < len(near):
            x_copies.append(z_start(0, send_x, recv_x, near[step]))
    s_copies += [z_start(1, send_s, recv_s, k) for k in near]
    z_own(send_x, recv_x)
    z_own(send_s, recv_s)

    g_passed = w_pass(0, full_g, g_direct)
    d_direct = w_start(2, wd_hbm, full_d)
    u_passed = w_pass(1, full_u, u_direct)
    hidden_units = wg_hbm.shape[2]
    arrived(x_copies)
    arrived(g_passed)
    own[4].wait()
    gate_act = dot(recv_x[...], full_g[...].reshape(width, hidden_units))
    d_passed = w_pass(2, full_d, d_direct)
    arrived(u_passed)
    own[5].wait()
    up_act = dot(recv_x[...], full_u[...].reshape(width, hidden_units))
    sigma = jax.nn.sigmoid(gate_act)
    hid_ref[...] = (gate_act * sigma * up_act).astype(BF16)
    fac_g[...] = up_act * sigma * (1.0 + gate_act * (1.0 - sigma))
    fac_u[...] = gate_act * sigma
    arrived(d_passed)
    own[6].wait()
    for q in range(n_dp):
        out_send[:, columns(q)] = dot(hid_ref[...], full_d[q]).astype(BF16)
    out_copies = [z_start(2, out_send, out_back, k) for k in far + near]
    z_own(out_send, out_back)

    arrived(s_copies)
    for q in range(n_dp):
        part_d[q] = dot_left_t(hid_ref[...], recv_s[:, columns(q)]).astype(BF16)
    pd_copies = g_start(2, part_d, got_d)
    backed = dot_right_t(recv_s[:, columns(0)], full_d[0])
    for q in range(1, n_dp):
        backed = backed + dot_right_t(recv_s[:, columns(q)], full_d[q])
    dg_ref[...] = (backed * fac_g[...]).astype(BF16)
    du_ref[...] = (backed * fac_u[...]).astype(BF16)
    for q in range(n_dp):
        part_g[q] = dot_left_t(recv_x[:, columns(q)], dg_ref[...]).astype(BF16)
    pg_copies = g_start(0, part_g, got_g)
    for q in range(n_dp):
        part_u[q] = dot_left_t(recv_x[:, columns(q)], du_ref[...]).astype(BF16)
    pu_copies = g_start(1, part_u, got_u)
    for q in range(n_dp):
        in_send[:, columns(q)] = (
            dot_right_t(dg_ref[...], full_g[q]) + dot_right_t(du_ref[...], full_u[q])
        ).astype(BF16)
    in_copies = [z_start(3, in_send, in_back, k) for k in far + near]
    z_own(in_send, in_back)
    g_pass(2, part_d, got_d, sum_d, pd_copies)
    g_pass(0, part_g, got_g, sum_g, pg_copies)
    g_pass(1, part_u, got_u, sum_u, pu_copies)

    arrived(out_copies)
    row_out = dot_left_t(place_ref[...], out_back[...])
    gated_ref[...] = (gates * row_out).astype(BF16)
    row_sums = jnp.sum(cot_ref[...].astype(F32) * row_out, 1, keepdims=True)
    ggrad_ref[...] = jnp.sum(jnp.where(diagonal, row_sums, 0.0), 0, keepdims=True)
    store(gated_ref, gated_hbm)
    store(ggrad_ref, ggrad_hbm)
    g_finish(part_d, got_d, pd_copies, ogd_ref)
    store(ogd_ref, ogd_hbm)
    g_finish(part_g, got_g, pg_copies, ogg_ref)
    store(ogg_ref, ogg_hbm)
    g_finish(part_u, got_u, pu_copies, ogu_ref)
    store(ogu_ref, ogu_hbm)
    arrived(in_copies)
    igrad_ref[...] = dot_left_t(place_ref[...], in_back[...]).astype(BF16)
    store(igrad_ref, igrad_hbm)
    for copy in copies:
        copy.wait_send()
    for copy in stored:
        copy.wait()


def results_kernel(*refs):
    count = len(refs) // 3
    sources, targets, held = refs[:count], refs[count : 2 * count], refs[2 * count : 3 * count]
    in_sem, out_sem = refs[3 * count :]
    reads = [pltpu.make_async_copy(sources[i], held[i], in_sem.at[i]) for i in range(count)]
    writes = [pltpu.make_async_copy(held[i], targets[i], out_sem.at[i]) for i in range(count)]
    for read in reads:
        read.start()
    for read, write in zip(reads, writes):
        read.wait()
        write.start()
    for write in writes:
        write.wait()


def power_of_two(size):
    return size & (size - 1) == 0


def per_device(x_rows, expert_ids, gates, cotangent, w_gate, w_up, w_down):
    n_dp, n_ex = lax.axis_size("dp"), lax.axis_size("expert")
    rows, width = x_rows.shape
    cap = 2 * rows // n_ex
    _, piece, hidden = w_gate.shape
    if cap % 16 or piece % 32 or hidden % 32 or not power_of_two(n_ex) or n_dp != 4:
        return collective_device(x_rows, expert_ids, gates, cotangent, w_gate, w_up, w_down)
    total = n_ex * cap
    hbm = pl.BlockSpec(memory_space=pltpu.HBM)
    slots_of = pltpu.VMEM((total, width), BF16)
    gates_of = pltpu.VMEM((n_dp, piece, hidden), BF16)
    downs_of = pltpu.VMEM((n_dp, hidden, piece), BF16)
    got_gates = pltpu.VMEM((6, piece // 2, hidden), BF16)
    got_downs = pltpu.VMEM((6, hidden // 2, piece), BF16)
    sum_gates = pltpu.VMEM((2, piece // 2, hidden), BF16)
    sum_downs = pltpu.VMEM((2, hidden // 2, piece), BF16)
    acts_of = pltpu.VMEM((total, hidden), BF16)
    facs_of = pltpu.VMEM((total, hidden), F32)
    shapes = (
        jax.ShapeDtypeStruct((rows, width), BF16),
        jax.ShapeDtypeStruct((rows, width), BF16),
        jax.ShapeDtypeStruct((1, rows), F32),
        jax.ShapeDtypeStruct(w_gate.shape, BF16),
        jax.ShapeDtypeStruct(w_up.shape, BF16),
        jax.ShapeDtypeStruct(w_down.shape, BF16),
    )
    results = pl.pallas_call(
        functools.partial(layer_kernel, n_dp, n_ex, cap),
        out_shape=shapes,
        in_specs=[hbm] * 7,
        out_specs=[hbm] * 6,
        scratch_shapes=[
            *(pltpu.VMEM(shape.shape, shape.dtype) for shape in shapes),
            pltpu.VMEM((rows, width), BF16), pltpu.VMEM((1, rows), jnp.int32),
            pltpu.VMEM((1, rows), F32), pltpu.VMEM((rows, width), BF16),
            pltpu.VMEM((total, rows), BF16),
            slots_of, slots_of, slots_of, slots_of, slots_of, slots_of, slots_of, slots_of,
            gates_of, gates_of, downs_of,
            acts_of, facs_of, facs_of, acts_of, acts_of,
            gates_of, gates_of, downs_of,
            got_gates, got_gates, got_downs, sum_gates, sum_gates, sum_downs,
            pltpu.SemaphoreType.DMA((7,)), pltpu.SemaphoreType.DMA((6,)),
            pltpu.SemaphoreType.DMA((4, n_ex)), pltpu.SemaphoreType.DMA((4, n_ex)),
            pltpu.SemaphoreType.DMA((3, 4)), pltpu.SemaphoreType.DMA((3, 4)),
            pltpu.SemaphoreType.DMA((3, 6)), pltpu.SemaphoreType.DMA((3, 6)),
        ],
        compiler_params=pltpu.CompilerParams(
            collective_id=0, has_side_effects=True, vmem_limit_bytes=64 * 1024 * 1024
        ),
    )(
        x_rows, expert_ids.reshape(1, rows), gates.reshape(1, rows), cotangent,
        w_gate, w_up, w_down,
    )
    results = pl.pallas_call(
        results_kernel,
        out_shape=shapes,
        in_specs=[hbm] * 6,
        out_specs=[hbm] * 6,
        scratch_shapes=[
            *(pltpu.VMEM(shape.shape, shape.dtype) for shape in shapes),
            pltpu.SemaphoreType.DMA((6,)), pltpu.SemaphoreType.DMA((6,)),
        ],
        compiler_params=pltpu.CompilerParams(vmem_limit_bytes=64 * 1024 * 1024),
    )(*results)
    return (*results[:2], results[2].reshape(rows, 1), *results[3:])


def solution(mesh):
    in_specs = (
        P(("dp", "expert"), None),
        P(("dp", "expert"), None),
        P(("dp", "expert"), None),
        P(("dp", "expert"), None),
        P("expert", "dp", None),
        P("expert", "dp", None),
        P("expert", None, "dp"),
    )
    out_specs = (
        P(("dp", "expert"), None),
        P(("dp", "expert"), None),
        P(("dp", "expert"), None),
        P("expert", "dp", None),
        P("expert", "dp", None),
        P("expert", None, "dp"),
    )
    return jax.shard_map(
        per_device, mesh=mesh, in_specs=in_specs, out_specs=out_specs, check_vma=False
    )
```

```python
import functools

import jax
import jax.numpy as jnp
from jax import lax
from jax.experimental import pallas as pl
from jax.experimental.pallas import tpu as pltpu
from jax.sharding import PartitionSpec as P


def expert_rows(rows_in, rows_scaled, proj_gate, proj_up, proj_down):
    gate_act = jnp.dot(rows_in, proj_gate, preferred_element_type=jnp.float32)
    up_act = jnp.dot(rows_in, proj_up, preferred_element_type=jnp.float32)
    sigma = jax.nn.sigmoid(gate_act)
    hidden = (gate_act * sigma * up_act).astype(jnp.bfloat16)
    result = jnp.dot(hidden, proj_down, preferred_element_type=jnp.float32).astype(jnp.bfloat16)
    backed = jnp.dot(rows_scaled, proj_down.T, preferred_element_type=jnp.float32)
    d_gate_act = (backed * up_act * sigma * (1.0 + gate_act * (1.0 - sigma))).astype(jnp.bfloat16)
    d_up_act = (backed * gate_act * sigma).astype(jnp.bfloat16)
    d_input = (
        jnp.dot(d_gate_act, proj_gate.T, preferred_element_type=jnp.float32)
        + jnp.dot(d_up_act, proj_up.T, preferred_element_type=jnp.float32)
    ).astype(jnp.bfloat16)
    grad_g = jnp.dot(rows_in.T, d_gate_act, preferred_element_type=jnp.float32)
    grad_u = jnp.dot(rows_in.T, d_up_act, preferred_element_type=jnp.float32)
    grad_d = jnp.dot(hidden.T, rows_scaled, preferred_element_type=jnp.float32)
    return (result, d_input, (grad_g, grad_u, grad_d), (hidden, d_gate_act, d_up_act))


def rounded_sum(total, term):
    kept = lax.optimization_barrier(term.astype(jnp.bfloat16))
    return total + kept.astype(jnp.float32)


def collective_device(x_rows, expert_ids, gates, cotangent, w_gate, w_up, w_down):
    full_gate, full_up, full_down = (
        lax.all_gather(w_gate, "dp", axis=1, tiled=True),
        lax.all_gather(w_up, "dp", axis=1, tiled=True),
        lax.all_gather(w_down, "dp", axis=2, tiled=True),
    )
    proj_gate = full_gate[0]
    proj_up = full_up[0]
    proj_down = full_down[0]
    experts = lax.axis_size("expert")
    row_count = x_rows.shape[0]
    width = x_rows.shape[1]
    capacity = 2 * row_count // experts
    row_ids = expert_ids[:, 0]
    onehot = (row_ids[:, None] == jnp.arange(experts, dtype=jnp.int32)[None, :]).astype(jnp.int32)
    ranking = jnp.sum((jnp.cumsum(onehot, 0) - onehot) * onehot, 1)
    slot = row_ids * capacity + ranking
    counts = jnp.sum(onehot, 0)
    scaled = (gates * cotangent.astype(jnp.float32)).astype(jnp.bfloat16)
    send_in = (
        jnp.zeros((experts * capacity, width), jnp.bfloat16)
        .at[slot]
        .set(x_rows)
        .reshape(experts, capacity, width)
    )
    send_scaled = (
        jnp.zeros((experts * capacity, width), jnp.bfloat16)
        .at[slot]
        .set(scaled)
        .reshape(experts, capacity, width)
    )
    recv_in, recv_scaled, recv_counts = (
        lax.all_to_all(send_in, "expert", split_axis=0, concat_axis=0, tiled=True),
        lax.all_to_all(send_scaled, "expert", split_axis=0, concat_axis=0, tiled=True),
        lax.all_to_all(
            counts.reshape(experts, 1), "expert", split_axis=0, concat_axis=0, tiled=True
        ),
    )
    flat_in = recv_in.reshape(experts * capacity, width)
    flat_scaled = recv_scaled.reshape(experts * capacity, width)
    slot_out, slot_grad, grads, acts = expert_rows(
        flat_in, flat_scaled, proj_gate, proj_up, proj_down
    )
    back_result, back_input = (
        lax.all_to_all(
            slot_out.reshape(experts, capacity, width),
            "expert",
            split_axis=0,
            concat_axis=0,
            tiled=True,
        ),
        lax.all_to_all(
            slot_grad.reshape(experts, capacity, width),
            "expert",
            split_axis=0,
            concat_axis=0,
            tiled=True,
        ),
    )
    row_out = back_result.reshape(experts * capacity, width)[slot]
    input_grad = back_input.reshape(experts * capacity, width)[slot]
    gated_out = (gates * row_out.astype(jnp.float32)).astype(jnp.bfloat16)
    gate_grad = jnp.sum(
        cotangent.astype(jnp.float32) * row_out.astype(jnp.float32), 1, keepdims=True
    )
    groups = lax.axis_size("dp")
    rows_here = flat_in.shape[0]
    slice_in, slice_scaled = (
        lax.all_to_all(flat_in, "dp", split_axis=1, concat_axis=0, tiled=True),
        lax.all_to_all(flat_scaled, "dp", split_axis=1, concat_axis=0, tiled=True),
    )
    all_hidden, all_dgate, all_dup = (
        lax.all_gather(acts[0], "dp", axis=0, tiled=True),
        lax.all_gather(acts[1], "dp", axis=0, tiled=True),
        lax.all_gather(acts[2], "dp", axis=0, tiled=True),
    )
    quarter = slice_in.shape[1]
    hidden_units = all_hidden.shape[1]
    total_gate = jnp.zeros((quarter, hidden_units), jnp.float32)
    total_up = jnp.zeros((quarter, hidden_units), jnp.float32)
    total_down = jnp.zeros((hidden_units, quarter), jnp.float32)
    for group in range(groups):
        first_row = group * rows_here
        group_in = slice_in[first_row : first_row + rows_here]
        group_scaled = slice_scaled[first_row : first_row + rows_here]
        group_hidden = all_hidden[first_row : first_row + rows_here]
        group_dgate = all_dgate[first_row : first_row + rows_here]
        group_dup = all_dup[first_row : first_row + rows_here]
        total_gate = rounded_sum(
            total_gate, jnp.dot(group_in.T, group_dgate, preferred_element_type=jnp.float32)
        )
        total_up = rounded_sum(
            total_up, jnp.dot(group_in.T, group_dup, preferred_element_type=jnp.float32)
        )
        total_down = rounded_sum(
            total_down, jnp.dot(group_hidden.T, group_scaled, preferred_element_type=jnp.float32)
        )
    summed_gate = total_gate[None]
    summed_up = total_up[None]
    summed_down = total_down[None]
    return (
        gated_out,
        input_grad,
        gate_grad,
        summed_gate.astype(jnp.bfloat16),
        summed_up.astype(jnp.bfloat16),
        summed_down.astype(jnp.bfloat16),
    )


F32 = jnp.float32
BF16 = jnp.bfloat16


def dot(a, b):
    return lax.dot_general(a, b, (((1,), (0,)), ((), ())), preferred_element_type=F32)


def dot_left_t(a, b):
    return lax.dot_general(a, b, (((0,), (0,)), ((), ())), preferred_element_type=F32)


def dot_right_t(a, b):
    return lax.dot_general(a, b, (((1,), (1,)), ((), ())), preferred_element_type=F32)


def flipped(index, bits, size):
    result, place = 0, 1
    while place < size:
        digit = (index // place) % 2
        result = result + ((digit + 1) % 2 if bits & place else digit) * place
        place *= 2
    return result


def layer_kernel(
    n_dp, n_ex, cap,
    x_hbm, ids_hbm, gates_hbm, cot_hbm, wg_hbm, wu_hbm, wd_hbm,
    gated_hbm, in_back, ggrad_hbm, ogg_hbm, ogu_hbm, ogd_hbm, place_hbm,
    gated_ref, ggrad_ref, ogg_ref, ogu_ref, ogd_ref, row_place,
    x_ref, ids_ref, gates_ref, cot_ref,
    place_ref, send_x, send_s, recv_x, recv_s, out_send, in_send, out_back,
    full_g, full_u, full_d, hid_ref, fac_g, fac_u, dg_ref, du_ref, x_turned, hid_turned,
    part_g, part_u, part_d, got_g, got_u, got_d, sum_g, sum_u, sum_d,
    own_sem, out_sem, z_send, z_recv, w_send, w_recv, g_send, g_recv,
):
    me_e, me_d = lax.axis_index("expert"), lax.axis_index("dp")
    z_peers = [(k, flipped(me_e, k, n_ex)) for k in range(n_ex - 1, 0, -1)]
    side, over, across = (flipped(me_d, k, n_dp) for k in (1, 2, 3))
    rows, width = x_ref.shape
    piece = width // n_dp

    barrier = pltpu.get_barrier_semaphore()
    for _, peer in z_peers:
        pl.semaphore_signal(barrier, inc=1, device_id={"expert": peer}, device_id_type=pl.DeviceIdType.MESH)
    for peer in (side, over):
        pl.semaphore_signal(barrier, inc=1, device_id={"dp": peer}, device_id_type=pl.DeviceIdType.MESH)

    own = []
    for source, target in (
        (ids_hbm, ids_ref), (x_hbm, x_ref), (gates_hbm, gates_ref), (cot_hbm, cot_ref),
        (wg_hbm.at[0], full_g.at[me_d]), (wu_hbm.at[0], full_u.at[me_d]), (wd_hbm.at[0], full_d.at[me_d]),
    ):
        copy = pltpu.make_async_copy(source, target, own_sem.at[len(own)])
        copy.start()
        own.append(copy)

    def columns(q):
        return slice(q * piece, (q + 1) * piece)

    copies = []

    def remote(source, target, send_sem, recv_sem, axis, peer):
        copy = pltpu.make_async_remote_copy(
            src_ref=source,
            dst_ref=target,
            send_sem=send_sem,
            recv_sem=recv_sem,
            device_id={axis: peer},
            device_id_type=pl.DeviceIdType.MESH,
        )
        copy.start()
        copies.append(copy)
        return copy

    def slots(index):
        return pl.ds(pl.multiple_of(index * cap, cap), cap)

    def z_start(which, source, target, k):
        peer = flipped(me_e, k, n_ex)
        return remote(
            source.at[slots(peer)], target.at[slots(me_e)],
            z_send.at[which, k], z_recv.at[which, k], "expert", peer,
        )

    def z_own(source, target):
        target[slots(me_e), :] = source[slots(me_e), :]

    def w_start(which, source, target):
        return [
            remote(
                source.at[0], target.at[me_d],
                w_send.at[which, k], w_recv.at[which, k], "dp", peer,
            )
            for k, peer in enumerate((side, over))
        ]

    def w_pass(which, target, direct):
        half = target.shape[1] // 2
        first, second = target.at[side, pl.ds(0, half)], target.at[over, pl.ds(half, half)]
        direct[0].wait_recv()
        one = remote(first, first, w_send.at[which, 2], w_recv.at[which, 2], "dp", over)
        direct[1].wait_recv()
        two = remote(second, second, w_send.at[which, 3], w_recv.at[which, 3], "dp", side)
        return [one, two]

    def g_start(which, part, got):
        half = part.shape[1] // 2
        upper, lower = pl.ds(0, half), pl.ds(half, half)
        made = {}
        for slot, source, peer in (
            (1, part.at[across, upper], side),
            (3, part.at[across, lower], over),
            (0, part.at[side, upper], side),
            (2, part.at[over, lower], over),
        ):
            made[slot] = remote(
                source, got.at[slot], g_send.at[which, slot], g_recv.at[which, slot], "dp", peer
            )
        return made

    def g_pass(which, part, got, total, made):
        half = part.shape[1] // 2
        for slot, peer, rows_of in ((1, over, pl.ds(0, half)), (3, side, pl.ds(half, half))):
            made[slot].wait_recv()
            index, later = slot // 2, 4 + slot // 2
            total[index] = (part[peer, rows_of].astype(F32) + got[slot].astype(F32)).astype(BF16)
            made[later] = remote(
                total.at[index], got.at[later], g_send.at[which, later], g_recv.at[which, later], "dp", peer
            )

    def g_finish(part, got, made, out):
        half = part.shape[1] // 2
        for slot, later, rows_of in ((0, 4, pl.ds(0, half)), (2, 5, pl.ds(half, half))):
            made[slot].wait_recv()
            made[later].wait_recv()
            out[0, rows_of] = (
                part[me_d, rows_of].astype(F32) + got[slot].astype(F32) + got[later].astype(F32)
            ).astype(BF16)

    stored = []

    def store(source, target):
        copy = pltpu.make_async_copy(source, target, out_sem.at[len(stored)])
        copy.start()
        stored.append(copy)

    def arrived(made):
        for copy in made:
            copy.wait_recv()

    far = [k for k in range(n_ex - 1, 0, -1) if k >= n_ex // 2]
    near = [k for k in range(n_ex - 1, 0, -1) if k < n_ex // 2]

    own[0].wait()
    ids = ids_ref[...]
    onehot = (ids == lax.broadcasted_iota(jnp.int32, (n_ex, rows), 0)).astype(F32)
    row_a = lax.broadcasted_iota(jnp.int32, (rows, rows), 0)
    row_b = lax.broadcasted_iota(jnp.int32, (rows, rows), 1)
    ranks = jnp.sum(dot(onehot.astype(BF16), (row_a < row_b).astype(BF16)) * onehot, 0, keepdims=True)
    slot = ids * cap + ranks.astype(jnp.int32)
    place_ref[...] = (slot == lax.broadcasted_iota(jnp.int32, (n_ex * cap, rows), 0)).astype(BF16)
    diagonal = row_a == row_b
    slot_of_row = jnp.sum(jnp.where(diagonal, slot, 0), 1, keepdims=True)
    row_place[...] = (slot_of_row == lax.broadcasted_iota(jnp.int32, (rows, n_ex * cap), 1)).astype(BF16)
    own[1].wait()
    send_x[...] = dot(place_ref[...], x_ref[...]).astype(BF16)

    pl.semaphore_wait(barrier, n_ex + 1)

    x_copies = [z_start(0, send_x, recv_x, k) for k in far]
    g_direct = w_start(0, wg_hbm, full_g)
    u_direct = w_start(1, wu_hbm, full_u)

    own[2].wait()
    own[3].wait()
    gates = jnp.sum(jnp.where(diagonal, gates_ref[...], 0.0), 1, keepdims=True)
    scaled = (gates * cot_ref[...].astype(F32)).astype(BF16)
    send_s[...] = dot(place_ref[...], scaled).astype(BF16)
    s_copies = []
    for step, k in enumerate(far):
        s_copies.append(z_start(1, send_s, recv_s, k))
        if step < len(near):
            x_copies.append(z_start(0, send_x, recv_x, near[step]))
    s_copies += [z_start(1, send_s, recv_s, k) for k in near]
    z_own(send_x, recv_x)
    z_own(send_s, recv_s)
    store(row_place, place_hbm)

    g_passed = w_pass(0, full_g, g_direct)
    d_direct = w_start(2, wd_hbm, full_d)
    u_passed = w_pass(1, full_u, u_direct)
    hidden_units = wg_hbm.shape[2]
    arrived(x_copies)
    arrived(g_passed)
    own[4].wait()
    gate_act = dot(recv_x[...], full_g[...].reshape(width, hidden_units))
    d_passed = w_pass(2, full_d, d_direct)
    arrived(u_passed)
    own[5].wait()
    up_act = dot(recv_x[...], full_u[...].reshape(width, hidden_units))
    sigma = jax.nn.sigmoid(gate_act)
    hid_ref[...] = (gate_act * sigma * up_act).astype(BF16)
    fac_g[...] = up_act * sigma * (1.0 + gate_act * (1.0 - sigma))
    fac_u[...] = gate_act * sigma
    arrived(d_passed)
    own[6].wait()
    for q in range(n_dp):
        out_send[:, columns(q)] = dot(hid_ref[...], full_d[q]).astype(BF16)
    out_copies = [z_start(2, out_send, out_back, k) for k in far + near]
    z_own(out_send, out_back)
    x_turned[...] = recv_x[...].T
    hid_turned[...] = hid_ref[...].T

    arrived(s_copies)
    for q in range(n_dp):
        part_d[q] = dot(hid_turned[...], recv_s[:, columns(q)]).astype(BF16)
    pd_copies = g_start(2, part_d, got_d)
    backed = dot_right_t(recv_s[:, columns(0)], full_d[0])
    for q in range(1, n_dp):
        backed = backed + dot_right_t(recv_s[:, columns(q)], full_d[q])
    dg_ref[...] = (backed * fac_g[...]).astype(BF16)
    du_ref[...] = (backed * fac_u[...]).astype(BF16)
    for q in range(n_dp):
        part_g[q] = dot(x_turned[columns(q), :], dg_ref[...]).astype(BF16)
    pg_copies = g_start(0, part_g, got_g)
    for q in range(n_dp):
        part_u[q] = dot(x_turned[columns(q), :], du_ref[...]).astype(BF16)
    pu_copies = g_start(1, part_u, got_u)
    for q in range(n_dp):
        in_send[:, columns(q)] = (
            dot_right_t(dg_ref[...], full_g[q]) + dot_right_t(du_ref[...], full_u[q])
        ).astype(BF16)
    in_copies = [z_start(3, in_send, in_back, k) for k in far + near]
    store(in_send.at[slots(me_e)], in_back.at[slots(me_e)])
    g_pass(2, part_d, got_d, sum_d, pd_copies)
    g_pass(0, part_g, got_g, sum_g, pg_copies)
    g_pass(1, part_u, got_u, sum_u, pu_copies)

    arrived(out_copies)
    row_out = dot(row_place[...], out_back[...])
    gated_ref[...] = (gates * row_out).astype(BF16)
    row_sums = jnp.sum(cot_ref[...].astype(F32) * row_out, 1, keepdims=True)
    ggrad_ref[...] = jnp.sum(jnp.where(diagonal, row_sums, 0.0), 0, keepdims=True)
    store(gated_ref, gated_hbm)
    store(ggrad_ref, ggrad_hbm)
    g_finish(part_d, got_d, pd_copies, ogd_ref)
    store(ogd_ref, ogd_hbm)
    g_finish(part_g, got_g, pg_copies, ogg_ref)
    store(ogg_ref, ogg_hbm)
    g_finish(part_u, got_u, pu_copies, ogu_ref)
    store(ogu_ref, ogu_hbm)
    arrived(in_copies)
    for copy in copies:
        copy.wait_send()
    for copy in stored:
        copy.wait()


def results_kernel(*refs):
    back_hbm, place_hbm, *sources = refs[:7]
    igrad_hbm, *targets = refs[7:13]
    back, place, igrad, *held = refs[13:21]
    in_sem, out_sem = refs[21:]
    first = [
        pltpu.make_async_copy(back_hbm, back, in_sem.at[5]),
        pltpu.make_async_copy(place_hbm, place, in_sem.at[6]),
    ]
    reads = [pltpu.make_async_copy(sources[i], held[i], in_sem.at[i]) for i in range(5)]
    writes = [pltpu.make_async_copy(held[i], targets[i], out_sem.at[i]) for i in range(5)]
    for read in first + reads:
        read.start()
    for read in first:
        read.wait()
    igrad[...] = dot(place[...], back[...]).astype(BF16)
    last = pltpu.make_async_copy(igrad, igrad_hbm, out_sem.at[5])
    last.start()
    for read, write in zip(reads, writes):
        read.wait()
        write.start()
    for write in writes + [last]:
        write.wait()


def power_of_two(size):
    return size & (size - 1) == 0


def per_device(x_rows, expert_ids, gates, cotangent, w_gate, w_up, w_down):
    n_dp, n_ex = lax.axis_size("dp"), lax.axis_size("expert")
    rows, width = x_rows.shape
    cap = 2 * rows // n_ex
    _, piece, hidden = w_gate.shape
    if cap % 16 or piece % 32 or hidden % 32 or not power_of_two(n_ex) or n_dp != 4:
        return collective_device(x_rows, expert_ids, gates, cotangent, w_gate, w_up, w_down)
    total = n_ex * cap
    hbm = pl.BlockSpec(memory_space=pltpu.HBM)
    slots_of = pltpu.VMEM((total, width), BF16)
    gates_of = pltpu.VMEM((n_dp, piece, hidden), BF16)
    downs_of = pltpu.VMEM((n_dp, hidden, piece), BF16)
    got_gates = pltpu.VMEM((6, piece // 2, hidden), BF16)
    got_downs = pltpu.VMEM((6, hidden // 2, piece), BF16)
    sum_gates = pltpu.VMEM((2, piece // 2, hidden), BF16)
    sum_downs = pltpu.VMEM((2, hidden // 2, piece), BF16)
    acts_of = pltpu.VMEM((total, hidden), BF16)
    facs_of = pltpu.VMEM((total, hidden), F32)
    shapes = (
        jax.ShapeDtypeStruct((rows, width), BF16),
        jax.ShapeDtypeStruct((1, rows), F32),
        jax.ShapeDtypeStruct(w_gate.shape, BF16),
        jax.ShapeDtypeStruct(w_up.shape, BF16),
        jax.ShapeDtypeStruct(w_down.shape, BF16),
    )
    back_shape = jax.ShapeDtypeStruct((total, width), BF16)
    place_shape = jax.ShapeDtypeStruct((rows, total), BF16)
    gated, back, *others, place = pl.pallas_call(
        functools.partial(layer_kernel, n_dp, n_ex, cap),
        out_shape=(shapes[0], back_shape, *shapes[1:], place_shape),
        in_specs=[hbm] * 7,
        out_specs=[hbm] * 7,
        scratch_shapes=[
            *(pltpu.VMEM(shape.shape, shape.dtype) for shape in (*shapes, place_shape)),
            pltpu.VMEM((rows, width), BF16), pltpu.VMEM((1, rows), jnp.int32),
            pltpu.VMEM((1, rows), F32), pltpu.VMEM((rows, width), BF16),
            pltpu.VMEM((total, rows), BF16),
            slots_of, slots_of, slots_of, slots_of, slots_of, slots_of, slots_of,
            gates_of, gates_of, downs_of,
            acts_of, facs_of, facs_of, acts_of, acts_of,
            pltpu.VMEM((width, total), BF16), pltpu.VMEM((hidden, total), BF16),
            gates_of, gates_of, downs_of,
            got_gates, got_gates, got_downs, sum_gates, sum_gates, sum_downs,
            pltpu.SemaphoreType.DMA((7,)), pltpu.SemaphoreType.DMA((7,)),
            pltpu.SemaphoreType.DMA((4, n_ex)), pltpu.SemaphoreType.DMA((4, n_ex)),
            pltpu.SemaphoreType.DMA((3, 4)), pltpu.SemaphoreType.DMA((3, 4)),
            pltpu.SemaphoreType.DMA((3, 6)), pltpu.SemaphoreType.DMA((3, 6)),
        ],
        compiler_params=pltpu.CompilerParams(
            collective_id=0, has_side_effects=True, vmem_limit_bytes=64 * 1024 * 1024
        ),
    )(
        x_rows, expert_ids.reshape(1, rows), gates.reshape(1, rows), cotangent,
        w_gate, w_up, w_down,
    )
    igrad_shape = jax.ShapeDtypeStruct((rows, width), BF16)
    input_grad, gated_out, gate_grad, *weight_grads = pl.pallas_call(
        results_kernel,
        out_shape=(igrad_shape, *shapes),
        in_specs=[hbm] * 7,
        out_specs=[hbm] * 6,
        scratch_shapes=[
            *(pltpu.VMEM(shape.shape, shape.dtype) for shape in (back_shape, place_shape, igrad_shape, *shapes)),
            pltpu.SemaphoreType.DMA((7,)), pltpu.SemaphoreType.DMA((6,)),
        ],
        compiler_params=pltpu.CompilerParams(vmem_limit_bytes=64 * 1024 * 1024),
    )(back, place, gated, *others)
    return (gated_out, input_grad, gate_grad.reshape(rows, 1), *weight_grads)


def solution(mesh):
    in_specs = (
        P(("dp", "expert"), None),
        P(("dp", "expert"), None),
        P(("dp", "expert"), None),
        P(("dp", "expert"), None),
        P("expert", "dp", None),
        P("expert", "dp", None),
        P("expert", None, "dp"),
    )
    out_specs = (
        P(("dp", "expert"), None),
        P(("dp", "expert"), None),
        P(("dp", "expert"), None),
        P("expert", "dp", None),
        P("expert", "dp", None),
        P("expert", None, "dp"),
    )
    return jax.shard_map(
        per_device, mesh=mesh, in_specs=in_specs, out_specs=out_specs, check_vma=False
    )
```

```python
import functools

import jax
import jax.numpy as jnp
from jax import lax
from jax.experimental import pallas as pl
from jax.experimental.pallas import tpu as pltpu
from jax.sharding import PartitionSpec as P


def expert_rows(rows_in, rows_scaled, proj_gate, proj_up, proj_down):
    gate_act = jnp.dot(rows_in, proj_gate, preferred_element_type=jnp.float32)
    up_act = jnp.dot(rows_in, proj_up, preferred_element_type=jnp.float32)
    sigma = jax.nn.sigmoid(gate_act)
    hidden = (gate_act * sigma * up_act).astype(jnp.bfloat16)
    result = jnp.dot(hidden, proj_down, preferred_element_type=jnp.float32).astype(jnp.bfloat16)
    backed = jnp.dot(rows_scaled, proj_down.T, preferred_element_type=jnp.float32)
    d_gate_act = (backed * up_act * sigma * (1.0 + gate_act * (1.0 - sigma))).astype(jnp.bfloat16)
    d_up_act = (backed * gate_act * sigma).astype(jnp.bfloat16)
    d_input = (
        jnp.dot(d_gate_act, proj_gate.T, preferred_element_type=jnp.float32)
        + jnp.dot(d_up_act, proj_up.T, preferred_element_type=jnp.float32)
    ).astype(jnp.bfloat16)
    grad_g = jnp.dot(rows_in.T, d_gate_act, preferred_element_type=jnp.float32)
    grad_u = jnp.dot(rows_in.T, d_up_act, preferred_element_type=jnp.float32)
    grad_d = jnp.dot(hidden.T, rows_scaled, preferred_element_type=jnp.float32)
    return (result, d_input, (grad_g, grad_u, grad_d), (hidden, d_gate_act, d_up_act))


def rounded_sum(total, term):
    kept = lax.optimization_barrier(term.astype(jnp.bfloat16))
    return total + kept.astype(jnp.float32)


def collective_device(x_rows, expert_ids, gates, cotangent, w_gate, w_up, w_down):
    full_gate, full_up, full_down = (
        lax.all_gather(w_gate, "dp", axis=1, tiled=True),
        lax.all_gather(w_up, "dp", axis=1, tiled=True),
        lax.all_gather(w_down, "dp", axis=2, tiled=True),
    )
    proj_gate = full_gate[0]
    proj_up = full_up[0]
    proj_down = full_down[0]
    experts = lax.axis_size("expert")
    row_count = x_rows.shape[0]
    width = x_rows.shape[1]
    capacity = 2 * row_count // experts
    row_ids = expert_ids[:, 0]
    onehot = (row_ids[:, None] == jnp.arange(experts, dtype=jnp.int32)[None, :]).astype(jnp.int32)
    ranking = jnp.sum((jnp.cumsum(onehot, 0) - onehot) * onehot, 1)
    slot = row_ids * capacity + ranking
    counts = jnp.sum(onehot, 0)
    scaled = (gates * cotangent.astype(jnp.float32)).astype(jnp.bfloat16)
    send_in = (
        jnp.zeros((experts * capacity, width), jnp.bfloat16)
        .at[slot]
        .set(x_rows)
        .reshape(experts, capacity, width)
    )
    send_scaled = (
        jnp.zeros((experts * capacity, width), jnp.bfloat16)
        .at[slot]
        .set(scaled)
        .reshape(experts, capacity, width)
    )
    recv_in, recv_scaled, recv_counts = (
        lax.all_to_all(send_in, "expert", split_axis=0, concat_axis=0, tiled=True),
        lax.all_to_all(send_scaled, "expert", split_axis=0, concat_axis=0, tiled=True),
        lax.all_to_all(
            counts.reshape(experts, 1), "expert", split_axis=0, concat_axis=0, tiled=True
        ),
    )
    flat_in = recv_in.reshape(experts * capacity, width)
    flat_scaled = recv_scaled.reshape(experts * capacity, width)
    slot_out, slot_grad, grads, acts = expert_rows(
        flat_in, flat_scaled, proj_gate, proj_up, proj_down
    )
    back_result, back_input = (
        lax.all_to_all(
            slot_out.reshape(experts, capacity, width),
            "expert",
            split_axis=0,
            concat_axis=0,
            tiled=True,
        ),
        lax.all_to_all(
            slot_grad.reshape(experts, capacity, width),
            "expert",
            split_axis=0,
            concat_axis=0,
            tiled=True,
        ),
    )
    row_out = back_result.reshape(experts * capacity, width)[slot]
    input_grad = back_input.reshape(experts * capacity, width)[slot]
    gated_out = (gates * row_out.astype(jnp.float32)).astype(jnp.bfloat16)
    gate_grad = jnp.sum(
        cotangent.astype(jnp.float32) * row_out.astype(jnp.float32), 1, keepdims=True
    )
    groups = lax.axis_size("dp")
    rows_here = flat_in.shape[0]
    slice_in, slice_scaled = (
        lax.all_to_all(flat_in, "dp", split_axis=1, concat_axis=0, tiled=True),
        lax.all_to_all(flat_scaled, "dp", split_axis=1, concat_axis=0, tiled=True),
    )
    all_hidden, all_dgate, all_dup = (
        lax.all_gather(acts[0], "dp", axis=0, tiled=True),
        lax.all_gather(acts[1], "dp", axis=0, tiled=True),
        lax.all_gather(acts[2], "dp", axis=0, tiled=True),
    )
    quarter = slice_in.shape[1]
    hidden_units = all_hidden.shape[1]
    total_gate = jnp.zeros((quarter, hidden_units), jnp.float32)
    total_up = jnp.zeros((quarter, hidden_units), jnp.float32)
    total_down = jnp.zeros((hidden_units, quarter), jnp.float32)
    for group in range(groups):
        first_row = group * rows_here
        group_in = slice_in[first_row : first_row + rows_here]
        group_scaled = slice_scaled[first_row : first_row + rows_here]
        group_hidden = all_hidden[first_row : first_row + rows_here]
        group_dgate = all_dgate[first_row : first_row + rows_here]
        group_dup = all_dup[first_row : first_row + rows_here]
        total_gate = rounded_sum(
            total_gate, jnp.dot(group_in.T, group_dgate, preferred_element_type=jnp.float32)
        )
        total_up = rounded_sum(
            total_up, jnp.dot(group_in.T, group_dup, preferred_element_type=jnp.float32)
        )
        total_down = rounded_sum(
            total_down, jnp.dot(group_hidden.T, group_scaled, preferred_element_type=jnp.float32)
        )
    summed_gate = total_gate[None]
    summed_up = total_up[None]
    summed_down = total_down[None]
    return (
        gated_out,
        input_grad,
        gate_grad,
        summed_gate.astype(jnp.bfloat16),
        summed_up.astype(jnp.bfloat16),
        summed_down.astype(jnp.bfloat16),
    )


F32 = jnp.float32
BF16 = jnp.bfloat16


def dot(a, b):
    return lax.dot_general(a, b, (((1,), (0,)), ((), ())), preferred_element_type=F32)


def dot_left_t(a, b):
    return lax.dot_general(a, b, (((0,), (0,)), ((), ())), preferred_element_type=F32)


def dot_right_t(a, b):
    return lax.dot_general(a, b, (((1,), (1,)), ((), ())), preferred_element_type=F32)


def flipped(index, bits, size):
    result, place = 0, 1
    while place < size:
        result = result + ((index // place) % 2 + (bits // place) % 2) % 2 * place
        place *= 2
    return result


def layer_kernel(
    n_dp, n_ex, cap,
    x_hbm, ids_hbm, gates_hbm, cot_hbm, wg_hbm, wu_hbm, wd_hbm,
    gated_hbm, in_back, ggrad_hbm, ogg_hbm, ogu_hbm, ogd_hbm, place_hbm,
    gated_ref, ggrad_ref, ogg_ref, ogu_ref, ogd_ref, row_place,
    x_ref, ids_ref, gates_ref, cot_ref,
    place_ref, send_x, send_s, recv_x, recv_s, out_send, in_send, out_back,
    full_g, full_u, full_d, hid_ref, fac_g, fac_u, dg_ref, du_ref, x_turned, hid_turned,
    part_g, part_u, part_d, got_g, got_u, got_d, sum_g, sum_u, sum_d,
    own_sem, out_sem, z_send, z_recv, w_send, w_recv, g_send, g_recv,
):
    me_e, me_d = lax.axis_index("expert"), lax.axis_index("dp")
    z_peers = [(k, flipped(me_e, k, n_ex)) for k in range(n_ex - 1, 0, -1)]
    side, over, across = (flipped(me_d, k, n_dp) for k in (1, 2, 3))
    rows, width = x_ref.shape
    piece = width // n_dp

    barrier = pltpu.get_barrier_semaphore()
    for _, peer in z_peers:
        pl.semaphore_signal(barrier, inc=1, device_id={"expert": peer}, device_id_type=pl.DeviceIdType.MESH)
    for peer in (side, over):
        pl.semaphore_signal(barrier, inc=1, device_id={"dp": peer}, device_id_type=pl.DeviceIdType.MESH)

    own = []
    for source, target in (
        (ids_hbm, ids_ref), (x_hbm, x_ref), (gates_hbm, gates_ref), (cot_hbm, cot_ref),
        (wg_hbm.at[0], full_g.at[me_d]), (wu_hbm.at[0], full_u.at[me_d]), (wd_hbm.at[0], full_d.at[me_d]),
    ):
        copy = pltpu.make_async_copy(source, target, own_sem.at[len(own)])
        copy.start()
        own.append(copy)

    def columns(q):
        return slice(q * piece, (q + 1) * piece)

    copies = []

    def remote(source, target, send_sem, recv_sem, axis, peer):
        copy = pltpu.make_async_remote_copy(
            src_ref=source,
            dst_ref=target,
            send_sem=send_sem,
            recv_sem=recv_sem,
            device_id={axis: peer},
            device_id_type=pl.DeviceIdType.MESH,
        )
        copy.start()
        copies.append(copy)
        return copy

    def slots(index):
        return pl.ds(pl.multiple_of(index * cap, cap), cap)

    quarter = n_ex // 4
    outer = 1 - (me_e // quarter + 1) // 2 % 2

    def z_partner(turn):
        last = n_ex - 2 - turn
        return (last + (n_ex // 2 - 1) * outer) % (n_ex - 1) + 1

    def z_copy(which, source, target, k):
        peer = flipped(me_e, k, n_ex)
        return pltpu.make_async_remote_copy(
            src_ref=source.at[slots(peer)],
            dst_ref=target.at[slots(me_e)],
            send_sem=z_send.at[which, k],
            recv_sem=z_recv.at[which, k],
            device_id={"expert": peer},
            device_id_type=pl.DeviceIdType.MESH,
        )

    def z_start(which, source, target):
        for turn in range(n_ex - 1):
            z_copy(which, source, target, z_partner(turn)).start()
        made = [z_copy(which, source, target, k) for k in range(1, n_ex)]
        copies.extend(made)
        return made

    def z_own(source, target):
        target[slots(me_e), :] = source[slots(me_e), :]

    def w_start(which, source, target):
        return [
            remote(
                source.at[0], target.at[me_d],
                w_send.at[which, k], w_recv.at[which, k], "dp", peer,
            )
            for k, peer in enumerate((side, over))
        ]

    def w_pass(which, target, direct):
        half = target.shape[1] // 2
        first, second = target.at[side, pl.ds(0, half)], target.at[over, pl.ds(half, half)]
        direct[0].wait_recv()
        one = remote(first, first, w_send.at[which, 2], w_recv.at[which, 2], "dp", over)
        direct[1].wait_recv()
        two = remote(second, second, w_send.at[which, 3], w_recv.at[which, 3], "dp", side)
        return [one, two]

    def g_start(which, part, got):
        half = part.shape[1] // 2
        upper, lower = pl.ds(0, half), pl.ds(half, half)
        made = {}
        for slot, source, peer in (
            (1, part.at[across, upper], side),
            (3, part.at[across, lower], over),
            (0, part.at[side, upper], side),
            (2, part.at[over, lower], over),
        ):
            made[slot] = remote(
                source, got.at[slot], g_send.at[which, slot], g_recv.at[which, slot], "dp", peer
            )
        return made

    def g_pass(which, part, got, total, made):
        half = part.shape[1] // 2
        for slot, peer, rows_of in ((1, over, pl.ds(0, half)), (3, side, pl.ds(half, half))):
            made[slot].wait_recv()
            index, later = slot // 2, 4 + slot // 2
            total[index] = (part[peer, rows_of].astype(F32) + got[slot].astype(F32)).astype(BF16)
            made[later] = remote(
                total.at[index], got.at[later], g_send.at[which, later], g_recv.at[which, later], "dp", peer
            )

    def g_finish(part, got, made, out):
        half = part.shape[1] // 2
        for slot, later, rows_of in ((0, 4, pl.ds(0, half)), (2, 5, pl.ds(half, half))):
            made[slot].wait_recv()
            made[later].wait_recv()
            out[0, rows_of] = (
                part[me_d, rows_of].astype(F32) + got[slot].astype(F32) + got[later].astype(F32)
            ).astype(BF16)

    stored = []

    def store(source, target):
        copy = pltpu.make_async_copy(source, target, out_sem.at[len(stored)])
        copy.start()
        stored.append(copy)

    def arrived(made):
        for copy in made:
            copy.wait_recv()

    own[0].wait()
    ids = ids_ref[...]
    onehot = (ids == lax.broadcasted_iota(jnp.int32, (n_ex, rows), 0)).astype(F32)
    row_a = lax.broadcasted_iota(jnp.int32, (rows, rows), 0)
    row_b = lax.broadcasted_iota(jnp.int32, (rows, rows), 1)
    ranks = jnp.sum(dot(onehot.astype(BF16), (row_a < row_b).astype(BF16)) * onehot, 0, keepdims=True)
    slot = ids * cap + ranks.astype(jnp.int32)
    place_ref[...] = (slot == lax.broadcasted_iota(jnp.int32, (n_ex * cap, rows), 0)).astype(BF16)
    diagonal = row_a == row_b
    slot_of_row = jnp.sum(jnp.where(diagonal, slot, 0), 1, keepdims=True)
    row_place[...] = (slot_of_row == lax.broadcasted_iota(jnp.int32, (rows, n_ex * cap), 1)).astype(BF16)
    own[1].wait()
    send_x[...] = dot(place_ref[...], x_ref[...]).astype(BF16)

    pl.semaphore_wait(barrier, n_ex + 1)

    x_copies = z_start(0, send_x, recv_x)
    g_direct = w_start(0, wg_hbm, full_g)
    u_direct = w_start(1, wu_hbm, full_u)

    own[2].wait()
    own[3].wait()
    gates = jnp.sum(jnp.where(diagonal, gates_ref[...], 0.0), 1, keepdims=True)
    scaled = (gates * cot_ref[...].astype(F32)).astype(BF16)
    send_s[...] = dot(place_ref[...], scaled).astype(BF16)
    s_copies = z_start(1, send_s, recv_s)
    z_own(send_x, recv_x)
    z_own(send_s, recv_s)
    store(row_place, place_hbm)

    g_passed = w_pass(0, full_g, g_direct)
    d_direct = w_start(2, wd_hbm, full_d)
    u_passed = w_pass(1, full_u, u_direct)
    hidden_units = wg_hbm.shape[2]
    arrived(x_copies)
    arrived(g_passed)
    own[4].wait()
    gate_act = dot(recv_x[...], full_g[...].reshape(width, hidden_units))
    d_passed = w_pass(2, full_d, d_direct)
    arrived(u_passed)
    own[5].wait()
    up_act = dot(recv_x[...], full_u[...].reshape(width, hidden_units))
    sigma = jax.nn.sigmoid(gate_act)
    hid_ref[...] = (gate_act * sigma * up_act).astype(BF16)
    fac_g[...] = up_act * sigma * (1.0 + gate_act * (1.0 - sigma))
    fac_u[...] = gate_act * sigma
    arrived(d_passed)
    own[6].wait()
    for q in range(n_dp):
        out_send[:, columns(q)] = dot(hid_ref[...], full_d[q]).astype(BF16)
    out_copies = z_start(2, out_send, out_back)
    z_own(out_send, out_back)
    x_turned[...] = recv_x[...].T
    hid_turned[...] = hid_ref[...].T

    arrived(s_copies)
    for q in range(n_dp):
        part_d[q] = dot(hid_turned[...], recv_s[:, columns(q)]).astype(BF16)
    pd_copies = g_start(2, part_d, got_d)
    backed = dot_right_t(recv_s[:, columns(0)], full_d[0])
    for q in range(1, n_dp):
        backed = backed + dot_right_t(recv_s[:, columns(q)], full_d[q])
    dg_ref[...] = (backed * fac_g[...]).astype(BF16)
    du_ref[...] = (backed * fac_u[...]).astype(BF16)
    for q in range(n_dp):
        part_g[q] = dot(x_turned[columns(q), :], dg_ref[...]).astype(BF16)
    pg_copies = g_start(0, part_g, got_g)
    for q in range(n_dp):
        part_u[q] = dot(x_turned[columns(q), :], du_ref[...]).astype(BF16)
    pu_copies = g_start(1, part_u, got_u)
    for q in range(n_dp):
        in_send[:, columns(q)] = (
            dot_right_t(dg_ref[...], full_g[q]) + dot_right_t(du_ref[...], full_u[q])
        ).astype(BF16)
    in_copies = z_start(3, in_send, in_back)
    store(in_send.at[slots(me_e)], in_back.at[slots(me_e)])
    g_pass(2, part_d, got_d, sum_d, pd_copies)
    g_pass(0, part_g, got_g, sum_g, pg_copies)
    g_pass(1, part_u, got_u, sum_u, pu_copies)

    arrived(out_copies)
    row_out = dot(row_place[...], out_back[...])
    gated_ref[...] = (gates * row_out).astype(BF16)
    row_sums = jnp.sum(cot_ref[...].astype(F32) * row_out, 1, keepdims=True)
    ggrad_ref[...] = jnp.sum(jnp.where(diagonal, row_sums, 0.0), 0, keepdims=True)
    store(gated_ref, gated_hbm)
    store(ggrad_ref, ggrad_hbm)
    g_finish(part_d, got_d, pd_copies, ogd_ref)
    store(ogd_ref, ogd_hbm)
    g_finish(part_g, got_g, pg_copies, ogg_ref)
    store(ogg_ref, ogg_hbm)
    g_finish(part_u, got_u, pu_copies, ogu_ref)
    store(ogu_ref, ogu_hbm)
    arrived(in_copies)
    for copy in copies:
        copy.wait_send()
    for copy in stored:
        copy.wait()


def results_kernel(*refs):
    back_hbm, place_hbm, *sources = refs[:7]
    igrad_hbm, *targets = refs[7:13]
    back, place, igrad, *held = refs[13:21]
    in_sem, out_sem = refs[21:]
    first = [
        pltpu.make_async_copy(back_hbm, back, in_sem.at[5]),
        pltpu.make_async_copy(place_hbm, place, in_sem.at[6]),
    ]
    reads = [pltpu.make_async_copy(sources[i], held[i], in_sem.at[i]) for i in range(5)]
    writes = [pltpu.make_async_copy(held[i], targets[i], out_sem.at[i]) for i in range(5)]
    for read in first + reads:
        read.start()
    for read in first:
        read.wait()
    igrad[...] = dot(place[...], back[...]).astype(BF16)
    last = pltpu.make_async_copy(igrad, igrad_hbm, out_sem.at[5])
    last.start()
    for read, write in zip(reads, writes):
        read.wait()
        write.start()
    for write in writes + [last]:
        write.wait()


def power_of_two(size):
    return size & (size - 1) == 0


def per_device(x_rows, expert_ids, gates, cotangent, w_gate, w_up, w_down):
    n_dp, n_ex = lax.axis_size("dp"), lax.axis_size("expert")
    rows, width = x_rows.shape
    cap = 2 * rows // n_ex
    _, piece, hidden = w_gate.shape
    if cap % 16 or piece % 32 or hidden % 32 or not power_of_two(n_ex) or n_ex < 4 or n_dp != 4:
        return collective_device(x_rows, expert_ids, gates, cotangent, w_gate, w_up, w_down)
    total = n_ex * cap
    hbm = pl.BlockSpec(memory_space=pltpu.HBM)
    slots_of = pltpu.VMEM((total, width), BF16)
    gates_of = pltpu.VMEM((n_dp, piece, hidden), BF16)
    downs_of = pltpu.VMEM((n_dp, hidden, piece), BF16)
    got_gates = pltpu.VMEM((6, piece // 2, hidden), BF16)
    got_downs = pltpu.VMEM((6, hidden // 2, piece), BF16)
    sum_gates = pltpu.VMEM((2, piece // 2, hidden), BF16)
    sum_downs = pltpu.VMEM((2, hidden // 2, piece), BF16)
    acts_of = pltpu.VMEM((total, hidden), BF16)
    facs_of = pltpu.VMEM((total, hidden), F32)
    shapes = (
        jax.ShapeDtypeStruct((rows, width), BF16),
        jax.ShapeDtypeStruct((1, rows), F32),
        jax.ShapeDtypeStruct(w_gate.shape, BF16),
        jax.ShapeDtypeStruct(w_up.shape, BF16),
        jax.ShapeDtypeStruct(w_down.shape, BF16),
    )
    back_shape = jax.ShapeDtypeStruct((total, width), BF16)
    place_shape = jax.ShapeDtypeStruct((rows, total), BF16)
    gated, back, *others, place = pl.pallas_call(
        functools.partial(layer_kernel, n_dp, n_ex, cap),
        out_shape=(shapes[0], back_shape, *shapes[1:], place_shape),
        in_specs=[hbm] * 7,
        out_specs=[hbm] * 7,
        scratch_shapes=[
            *(pltpu.VMEM(shape.shape, shape.dtype) for shape in (*shapes, place_shape)),
            pltpu.VMEM((rows, width), BF16), pltpu.VMEM((1, rows), jnp.int32),
            pltpu.VMEM((1, rows), F32), pltpu.VMEM((rows, width), BF16),
            pltpu.VMEM((total, rows), BF16),
            slots_of, slots_of, slots_of, slots_of, slots_of, slots_of, slots_of,
            gates_of, gates_of, downs_of,
            acts_of, facs_of, facs_of, acts_of, acts_of,
            pltpu.VMEM((width, total), BF16), pltpu.VMEM((hidden, total), BF16),
            gates_of, gates_of, downs_of,
            got_gates, got_gates, got_downs, sum_gates, sum_gates, sum_downs,
            pltpu.SemaphoreType.DMA((7,)), pltpu.SemaphoreType.DMA((7,)),
            pltpu.SemaphoreType.DMA((4, n_ex)), pltpu.SemaphoreType.DMA((4, n_ex)),
            pltpu.SemaphoreType.DMA((3, 4)), pltpu.SemaphoreType.DMA((3, 4)),
            pltpu.SemaphoreType.DMA((3, 6)), pltpu.SemaphoreType.DMA((3, 6)),
        ],
        compiler_params=pltpu.CompilerParams(
            collective_id=0, has_side_effects=True, vmem_limit_bytes=64 * 1024 * 1024
        ),
    )(
        x_rows, expert_ids.reshape(1, rows), gates.reshape(1, rows), cotangent,
        w_gate, w_up, w_down,
    )
    igrad_shape = jax.ShapeDtypeStruct((rows, width), BF16)
    input_grad, gated_out, gate_grad, *weight_grads = pl.pallas_call(
        results_kernel,
        out_shape=(igrad_shape, *shapes),
        in_specs=[hbm] * 7,
        out_specs=[hbm] * 6,
        scratch_shapes=[
            *(pltpu.VMEM(shape.shape, shape.dtype) for shape in (back_shape, place_shape, igrad_shape, *shapes)),
            pltpu.SemaphoreType.DMA((7,)), pltpu.SemaphoreType.DMA((6,)),
        ],
        compiler_params=pltpu.CompilerParams(vmem_limit_bytes=64 * 1024 * 1024),
    )(back, place, gated, *others)
    return (gated_out, input_grad, gate_grad.reshape(rows, 1), *weight_grads)


def solution(mesh):
    in_specs = (
        P(("dp", "expert"), None),
        P(("dp", "expert"), None),
        P(("dp", "expert"), None),
        P(("dp", "expert"), None),
        P("expert", "dp", None),
        P("expert", "dp", None),
        P("expert", None, "dp"),
    )
    out_specs = (
        P(("dp", "expert"), None),
        P(("dp", "expert"), None),
        P(("dp", "expert"), None),
        P("expert", "dp", None),
        P("expert", "dp", None),
        P("expert", None, "dp"),
    )
    return jax.shard_map(
        per_device, mesh=mesh, in_specs=in_specs, out_specs=out_specs, check_vma=False
    )
```

```python
import functools

import jax
import jax.numpy as jnp
from jax import lax
from jax.experimental import pallas as pl
from jax.experimental.pallas import tpu as pltpu
from jax.sharding import PartitionSpec as P


def expert_rows(rows_in, rows_scaled, proj_gate, proj_up, proj_down):
    gate_act = jnp.dot(rows_in, proj_gate, preferred_element_type=jnp.float32)
    up_act = jnp.dot(rows_in, proj_up, preferred_element_type=jnp.float32)
    sigma = jax.nn.sigmoid(gate_act)
    hidden = (gate_act * sigma * up_act).astype(jnp.bfloat16)
    result = jnp.dot(hidden, proj_down, preferred_element_type=jnp.float32).astype(jnp.bfloat16)
    backed = jnp.dot(rows_scaled, proj_down.T, preferred_element_type=jnp.float32)
    d_gate_act = (backed * up_act * sigma * (1.0 + gate_act * (1.0 - sigma))).astype(jnp.bfloat16)
    d_up_act = (backed * gate_act * sigma).astype(jnp.bfloat16)
    d_input = (
        jnp.dot(d_gate_act, proj_gate.T, preferred_element_type=jnp.float32)
        + jnp.dot(d_up_act, proj_up.T, preferred_element_type=jnp.float32)
    ).astype(jnp.bfloat16)
    grad_g = jnp.dot(rows_in.T, d_gate_act, preferred_element_type=jnp.float32)
    grad_u = jnp.dot(rows_in.T, d_up_act, preferred_element_type=jnp.float32)
    grad_d = jnp.dot(hidden.T, rows_scaled, preferred_element_type=jnp.float32)
    return (result, d_input, (grad_g, grad_u, grad_d), (hidden, d_gate_act, d_up_act))


def rounded_sum(total, term):
    kept = lax.optimization_barrier(term.astype(jnp.bfloat16))
    return total + kept.astype(jnp.float32)


def collective_device(x_rows, expert_ids, gates, cotangent, w_gate, w_up, w_down):
    full_gate, full_up, full_down = (
        lax.all_gather(w_gate, "dp", axis=1, tiled=True),
        lax.all_gather(w_up, "dp", axis=1, tiled=True),
        lax.all_gather(w_down, "dp", axis=2, tiled=True),
    )
    proj_gate = full_gate[0]
    proj_up = full_up[0]
    proj_down = full_down[0]
    experts = lax.axis_size("expert")
    row_count = x_rows.shape[0]
    width = x_rows.shape[1]
    capacity = 2 * row_count // experts
    row_ids = expert_ids[:, 0]
    onehot = (row_ids[:, None] == jnp.arange(experts, dtype=jnp.int32)[None, :]).astype(jnp.int32)
    ranking = jnp.sum((jnp.cumsum(onehot, 0) - onehot) * onehot, 1)
    slot = row_ids * capacity + ranking
    counts = jnp.sum(onehot, 0)
    scaled = (gates * cotangent.astype(jnp.float32)).astype(jnp.bfloat16)
    send_in = (
        jnp.zeros((experts * capacity, width), jnp.bfloat16)
        .at[slot]
        .set(x_rows)
        .reshape(experts, capacity, width)
    )
    send_scaled = (
        jnp.zeros((experts * capacity, width), jnp.bfloat16)
        .at[slot]
        .set(scaled)
        .reshape(experts, capacity, width)
    )
    recv_in, recv_scaled, recv_counts = (
        lax.all_to_all(send_in, "expert", split_axis=0, concat_axis=0, tiled=True),
        lax.all_to_all(send_scaled, "expert", split_axis=0, concat_axis=0, tiled=True),
        lax.all_to_all(
            counts.reshape(experts, 1), "expert", split_axis=0, concat_axis=0, tiled=True
        ),
    )
    flat_in = recv_in.reshape(experts * capacity, width)
    flat_scaled = recv_scaled.reshape(experts * capacity, width)
    slot_out, slot_grad, grads, acts = expert_rows(
        flat_in, flat_scaled, proj_gate, proj_up, proj_down
    )
    back_result, back_input = (
        lax.all_to_all(
            slot_out.reshape(experts, capacity, width),
            "expert",
            split_axis=0,
            concat_axis=0,
            tiled=True,
        ),
        lax.all_to_all(
            slot_grad.reshape(experts, capacity, width),
            "expert",
            split_axis=0,
            concat_axis=0,
            tiled=True,
        ),
    )
    row_out = back_result.reshape(experts * capacity, width)[slot]
    input_grad = back_input.reshape(experts * capacity, width)[slot]
    gated_out = (gates * row_out.astype(jnp.float32)).astype(jnp.bfloat16)
    gate_grad = jnp.sum(
        cotangent.astype(jnp.float32) * row_out.astype(jnp.float32), 1, keepdims=True
    )
    groups = lax.axis_size("dp")
    rows_here = flat_in.shape[0]
    slice_in, slice_scaled = (
        lax.all_to_all(flat_in, "dp", split_axis=1, concat_axis=0, tiled=True),
        lax.all_to_all(flat_scaled, "dp", split_axis=1, concat_axis=0, tiled=True),
    )
    all_hidden, all_dgate, all_dup = (
        lax.all_gather(acts[0], "dp", axis=0, tiled=True),
        lax.all_gather(acts[1], "dp", axis=0, tiled=True),
        lax.all_gather(acts[2], "dp", axis=0, tiled=True),
    )
    quarter = slice_in.shape[1]
    hidden_units = all_hidden.shape[1]
    total_gate = jnp.zeros((quarter, hidden_units), jnp.float32)
    total_up = jnp.zeros((quarter, hidden_units), jnp.float32)
    total_down = jnp.zeros((hidden_units, quarter), jnp.float32)
    for group in range(groups):
        first_row = group * rows_here
        group_in = slice_in[first_row : first_row + rows_here]
        group_scaled = slice_scaled[first_row : first_row + rows_here]
        group_hidden = all_hidden[first_row : first_row + rows_here]
        group_dgate = all_dgate[first_row : first_row + rows_here]
        group_dup = all_dup[first_row : first_row + rows_here]
        total_gate = rounded_sum(
            total_gate, jnp.dot(group_in.T, group_dgate, preferred_element_type=jnp.float32)
        )
        total_up = rounded_sum(
            total_up, jnp.dot(group_in.T, group_dup, preferred_element_type=jnp.float32)
        )
        total_down = rounded_sum(
            total_down, jnp.dot(group_hidden.T, group_scaled, preferred_element_type=jnp.float32)
        )
    summed_gate = total_gate[None]
    summed_up = total_up[None]
    summed_down = total_down[None]
    return (
        gated_out,
        input_grad,
        gate_grad,
        summed_gate.astype(jnp.bfloat16),
        summed_up.astype(jnp.bfloat16),
        summed_down.astype(jnp.bfloat16),
    )


F32 = jnp.float32
BF16 = jnp.bfloat16


def dot(a, b):
    return lax.dot_general(a, b, (((1,), (0,)), ((), ())), preferred_element_type=F32)


def dot_left_t(a, b):
    return lax.dot_general(a, b, (((0,), (0,)), ((), ())), preferred_element_type=F32)


def dot_right_t(a, b):
    return lax.dot_general(a, b, (((1,), (1,)), ((), ())), preferred_element_type=F32)


def flipped(index, bits, size):
    result, place = 0, 1
    while place < size:
        digit = (index // place) % 2
        result = result + ((digit + 1) % 2 if bits & place else digit) * place
        place *= 2
    return result


def layer_kernel(
    n_dp, n_ex, cap,
    x_hbm, ids_hbm, gates_hbm, cot_hbm, wg_hbm, wu_hbm, wd_hbm,
    gated_hbm, in_back, ggrad_hbm, ogg_hbm, ogu_hbm, ogd_hbm, place_hbm,
    gated_ref, ggrad_ref, ogg_ref, ogu_ref, ogd_ref, row_place,
    x_ref, ids_ref, gates_ref, cot_ref,
    place_ref, send_x, send_s, recv_x, recv_s, out_send, in_send, out_back,
    full_g, full_u, full_d, hid_ref, fac_g, fac_u, dg_ref, du_ref, x_turned, hid_turned,
    part_g, part_u, part_d, got_g, got_u, got_d, sum_g, sum_u, sum_d,
    own_sem, out_sem, z_send, z_recv, w_send, w_recv, g_send, g_recv,
):
    me_e, me_d = lax.axis_index("expert"), lax.axis_index("dp")
    z_peers = [(k, flipped(me_e, k, n_ex)) for k in range(n_ex - 1, 0, -1)]
    side, over, across = (flipped(me_d, k, n_dp) for k in (1, 2, 3))
    rows, width = x_ref.shape
    piece = width // n_dp

    barrier = pltpu.get_barrier_semaphore()
    for _, peer in z_peers:
        pl.semaphore_signal(barrier, inc=1, device_id={"expert": peer}, device_id_type=pl.DeviceIdType.MESH)
    for peer in (side, over):
        pl.semaphore_signal(barrier, inc=1, device_id={"dp": peer}, device_id_type=pl.DeviceIdType.MESH)

    own = []
    for source, target in (
        (ids_hbm, ids_ref), (x_hbm, x_ref), (gates_hbm, gates_ref), (cot_hbm, cot_ref),
        (wg_hbm.at[0], full_g.at[me_d]), (wu_hbm.at[0], full_u.at[me_d]), (wd_hbm.at[0], full_d.at[me_d]),
    ):
        copy = pltpu.make_async_copy(source, target, own_sem.at[len(own)])
        copy.start()
        own.append(copy)

    def columns(q):
        return slice(q * piece, (q + 1) * piece)

    copies = []

    def remote(source, target, send_sem, recv_sem, axis, peer):
        copy = pltpu.make_async_remote_copy(
            src_ref=source,
            dst_ref=target,
            send_sem=send_sem,
            recv_sem=recv_sem,
            device_id={axis: peer},
            device_id_type=pl.DeviceIdType.MESH,
        )
        copy.start()
        copies.append(copy)
        return copy

    def slots(index):
        return pl.ds(pl.multiple_of(index * cap, cap), cap)

    def z_start(which, source, target, k):
        peer = flipped(me_e, k, n_ex)
        return remote(
            source.at[slots(peer)], target.at[slots(me_e)],
            z_send.at[which, k], z_recv.at[which, k], "expert", peer,
        )

    def z_own(source, target):
        target[slots(me_e), :] = source[slots(me_e), :]

    def w_start(which, source, target):
        return [
            remote(
                source.at[0], target.at[me_d],
                w_send.at[which, k], w_recv.at[which, k], "dp", peer,
            )
            for k, peer in enumerate((side, over))
        ]

    def w_pass(which, target, direct):
        half = target.shape[1] // 2
        first, second = target.at[side, pl.ds(0, half)], target.at[over, pl.ds(half, half)]
        direct[0].wait_recv()
        one = remote(first, first, w_send.at[which, 2], w_recv.at[which, 2], "dp", over)
        direct[1].wait_recv()
        two = remote(second, second, w_send.at[which, 3], w_recv.at[which, 3], "dp", side)
        return [one, two]

    def g_start(which, part, got):
        half = part.shape[1] // 2
        upper, lower = pl.ds(0, half), pl.ds(half, half)
        made = {}
        for slot, source, peer in (
            (1, part.at[across, upper], side),
            (3, part.at[across, lower], over),
            (0, part.at[side, upper], side),
            (2, part.at[over, lower], over),
        ):
            made[slot] = remote(
                source, got.at[slot], g_send.at[which, slot], g_recv.at[which, slot], "dp", peer
            )
        return made

    def g_pass(which, part, got, total, made):
        half = part.shape[1] // 2
        for slot, peer, rows_of in ((1, over, pl.ds(0, half)), (3, side, pl.ds(half, half))):
            made[slot].wait_recv()
            index, later = slot // 2, 4 + slot // 2
            total[index] = (part[peer, rows_of].astype(F32) + got[slot].astype(F32)).astype(BF16)
            made[later] = remote(
                total.at[index], got.at[later], g_send.at[which, later], g_recv.at[which, later], "dp", peer
            )

    def g_finish(part, got, made, out):
        half = part.shape[1] // 2
        for slot, later, rows_of in ((0, 4, pl.ds(0, half)), (2, 5, pl.ds(half, half))):
            made[slot].wait_recv()
            made[later].wait_recv()
            out[0, rows_of] = (
                part[me_d, rows_of].astype(F32) + got[slot].astype(F32) + got[later].astype(F32)
            ).astype(BF16)

    stored = []

    def store(source, target):
        copy = pltpu.make_async_copy(source, target, out_sem.at[len(stored)])
        copy.start()
        stored.append(copy)

    def arrived(made):
        for copy in made:
            copy.wait_recv()

    far = [k for k in range(n_ex - 1, 0, -1) if k >= n_ex // 2]
    near = [k for k in range(n_ex - 1, 0, -1) if k < n_ex // 2]

    own[0].wait()
    ids = ids_ref[...]
    onehot = (ids == lax.broadcasted_iota(jnp.int32, (n_ex, rows), 0)).astype(F32)
    row_a = lax.broadcasted_iota(jnp.int32, (rows, rows), 0)
    row_b = lax.broadcasted_iota(jnp.int32, (rows, rows), 1)
    ranks = jnp.sum(dot(onehot.astype(BF16), (row_a < row_b).astype(BF16)) * onehot, 0, keepdims=True)
    slot = ids * cap + ranks.astype(jnp.int32)
    place_ref[...] = (slot == lax.broadcasted_iota(jnp.int32, (n_ex * cap, rows), 0)).astype(BF16)
    own[1].wait()
    send_x[...] = dot(place_ref[...], x_ref[...]).astype(BF16)

    pl.semaphore_wait(barrier, n_ex + 1)

    x_far = [z_start(0, send_x, recv_x, k) for k in far]
    g_direct = w_start(0, wg_hbm, full_g)
    u_direct = w_start(1, wu_hbm, full_u)
    x_near = [z_start(0, send_x, recv_x, k) for k in near]

    own[2].wait()
    own[3].wait()
    diagonal = row_a == row_b
    gates = jnp.sum(jnp.where(diagonal, gates_ref[...], 0.0), 1, keepdims=True)
    scaled = (gates * cot_ref[...].astype(F32)).astype(BF16)
    send_s[...] = dot(place_ref[...], scaled).astype(BF16)
    s_copies = [z_start(1, send_s, recv_s, k) for k in near]
    slot_of_row = jnp.sum(jnp.where(diagonal, slot, 0), 1, keepdims=True)
    row_place[...] = (slot_of_row == lax.broadcasted_iota(jnp.int32, (rows, n_ex * cap), 1)).astype(BF16)
    z_own(send_x, recv_x)
    z_own(send_s, recv_s)
    store(row_place, place_hbm)

    g_passed = w_pass(0, full_g, g_direct)
    d_direct = w_start(2, wd_hbm, full_d)
    s_copies.append(z_start(1, send_s, recv_s, far[0]))
    u_passed = w_pass(1, full_u, u_direct)
    for copy in x_far:
        copy.wait_send()
        copies.remove(copy)
    s_copies += [z_start(1, send_s, recv_s, k) for k in far[1:]]
    hidden_units = wg_hbm.shape[2]
    arrived(x_far + x_near)
    arrived(g_passed)
    own[4].wait()
    gate_act = dot(recv_x[...], full_g[...].reshape(width, hidden_units))
    d_passed = w_pass(2, full_d, d_direct)
    arrived(u_passed)
    own[5].wait()
    up_act = dot(recv_x[...], full_u[...].reshape(width, hidden_units))
    sigma = jax.nn.sigmoid(gate_act)
    hid_ref[...] = (gate_act * sigma * up_act).astype(BF16)
    fac_g[...] = up_act * sigma * (1.0 + gate_act * (1.0 - sigma))
    fac_u[...] = gate_act * sigma
    arrived(d_passed)
    own[6].wait()
    for q in range(n_dp):
        out_send[:, columns(q)] = dot(hid_ref[...], full_d[q]).astype(BF16)
    out_copies = [z_start(2, out_send, out_back, k) for k in far + near]
    z_own(out_send, out_back)
    x_turned[...] = recv_x[...].T
    hid_turned[...] = hid_ref[...].T

    arrived(s_copies)
    for q in range(n_dp):
        part_d[q] = dot(hid_turned[...], recv_s[:, columns(q)]).astype(BF16)
    pd_copies = g_start(2, part_d, got_d)
    backed = dot_right_t(recv_s[:, columns(0)], full_d[0])
    for q in range(1, n_dp):
        backed = backed + dot_right_t(recv_s[:, columns(q)], full_d[q])
    dg_ref[...] = (backed * fac_g[...]).astype(BF16)
    du_ref[...] = (backed * fac_u[...]).astype(BF16)
    for q in range(n_dp):
        part_g[q] = dot(x_turned[columns(q), :], dg_ref[...]).astype(BF16)
    pg_copies = g_start(0, part_g, got_g)
    for q in range(n_dp):
        part_u[q] = dot(x_turned[columns(q), :], du_ref[...]).astype(BF16)
    pu_copies = g_start(1, part_u, got_u)
    for q in range(n_dp):
        in_send[:, columns(q)] = (
            dot_right_t(dg_ref[...], full_g[q]) + dot_right_t(du_ref[...], full_u[q])
        ).astype(BF16)
    in_copies = [z_start(3, in_send, in_back, k) for k in far + near]
    store(in_send.at[slots(me_e)], in_back.at[slots(me_e)])
    g_pass(2, part_d, got_d, sum_d, pd_copies)
    g_pass(0, part_g, got_g, sum_g, pg_copies)
    g_pass(1, part_u, got_u, sum_u, pu_copies)

    arrived(out_copies)
    row_out = dot(row_place[...], out_back[...])
    gated_ref[...] = (gates * row_out).astype(BF16)
    row_sums = jnp.sum(cot_ref[...].astype(F32) * row_out, 1, keepdims=True)
    ggrad_ref[...] = jnp.sum(jnp.where(diagonal, row_sums, 0.0), 0, keepdims=True)
    store(gated_ref, gated_hbm)
    store(ggrad_ref, ggrad_hbm)
    g_finish(part_d, got_d, pd_copies, ogd_ref)
    store(ogd_ref, ogd_hbm)
    g_finish(part_g, got_g, pg_copies, ogg_ref)
    store(ogg_ref, ogg_hbm)
    g_finish(part_u, got_u, pu_copies, ogu_ref)
    store(ogu_ref, ogu_hbm)
    arrived(in_copies)
    for copy in copies:
        copy.wait_send()
    for copy in stored:
        copy.wait()


def results_kernel(*refs):
    back_hbm, place_hbm, *sources = refs[:7]
    igrad_hbm, *targets = refs[7:13]
    back, place, igrad, *held = refs[13:21]
    in_sem, out_sem = refs[21:]
    first = [
        pltpu.make_async_copy(back_hbm, back, in_sem.at[5]),
        pltpu.make_async_copy(place_hbm, place, in_sem.at[6]),
    ]
    reads = [pltpu.make_async_copy(sources[i], held[i], in_sem.at[i]) for i in range(5)]
    writes = [pltpu.make_async_copy(held[i], targets[i], out_sem.at[i]) for i in range(5)]
    for read in first + reads:
        read.start()
    for read in first:
        read.wait()
    igrad[...] = dot(place[...], back[...]).astype(BF16)
    last = pltpu.make_async_copy(igrad, igrad_hbm, out_sem.at[5])
    last.start()
    for read, write in zip(reads, writes):
        read.wait()
        write.start()
    for write in writes + [last]:
        write.wait()


def power_of_two(size):
    return size & (size - 1) == 0


def per_device(x_rows, expert_ids, gates, cotangent, w_gate, w_up, w_down):
    n_dp, n_ex = lax.axis_size("dp"), lax.axis_size("expert")
    rows, width = x_rows.shape
    cap = 2 * rows // n_ex
    _, piece, hidden = w_gate.shape
    if cap % 16 or piece % 32 or hidden % 32 or not power_of_two(n_ex) or n_ex < 4 or n_dp != 4:
        return collective_device(x_rows, expert_ids, gates, cotangent, w_gate, w_up, w_down)
    total = n_ex * cap
    hbm = pl.BlockSpec(memory_space=pltpu.HBM)
    slots_of = pltpu.VMEM((total, width), BF16)
    gates_of = pltpu.VMEM((n_dp, piece, hidden), BF16)
    downs_of = pltpu.VMEM((n_dp, hidden, piece), BF16)
    got_gates = pltpu.VMEM((6, piece // 2, hidden), BF16)
    got_downs = pltpu.VMEM((6, hidden // 2, piece), BF16)
    sum_gates = pltpu.VMEM((2, piece // 2, hidden), BF16)
    sum_downs = pltpu.VMEM((2, hidden // 2, piece), BF16)
    acts_of = pltpu.VMEM((total, hidden), BF16)
    facs_of = pltpu.VMEM((total, hidden), F32)
    shapes = (
        jax.ShapeDtypeStruct((rows, width), BF16),
        jax.ShapeDtypeStruct((1, rows), F32),
        jax.ShapeDtypeStruct(w_gate.shape, BF16),
        jax.ShapeDtypeStruct(w_up.shape, BF16),
        jax.ShapeDtypeStruct(w_down.shape, BF16),
    )
    back_shape = jax.ShapeDtypeStruct((total, width), BF16)
    place_shape = jax.ShapeDtypeStruct((rows, total), BF16)
    gated, back, *others, place = pl.pallas_call(
        functools.partial(layer_kernel, n_dp, n_ex, cap),
        out_shape=(shapes[0], back_shape, *shapes[1:], place_shape),
        in_specs=[hbm] * 7,
        out_specs=[hbm] * 7,
        scratch_shapes=[
            *(pltpu.VMEM(shape.shape, shape.dtype) for shape in (*shapes, place_shape)),
            pltpu.VMEM((rows, width), BF16), pltpu.VMEM((1, rows), jnp.int32),
            pltpu.VMEM((1, rows), F32), pltpu.VMEM((rows, width), BF16),
            pltpu.VMEM((total, rows), BF16),
            slots_of, slots_of, slots_of, slots_of, slots_of, slots_of, slots_of,
            gates_of, gates_of, downs_of,
            acts_of, facs_of, facs_of, acts_of, acts_of,
            pltpu.VMEM((width, total), BF16), pltpu.VMEM((hidden, total), BF16),
            gates_of, gates_of, downs_of,
            got_gates, got_gates, got_downs, sum_gates, sum_gates, sum_downs,
            pltpu.SemaphoreType.DMA((7,)), pltpu.SemaphoreType.DMA((7,)),
            pltpu.SemaphoreType.DMA((4, n_ex)), pltpu.SemaphoreType.DMA((4, n_ex)),
            pltpu.SemaphoreType.DMA((3, 4)), pltpu.SemaphoreType.DMA((3, 4)),
            pltpu.SemaphoreType.DMA((3, 6)), pltpu.SemaphoreType.DMA((3, 6)),
        ],
        compiler_params=pltpu.CompilerParams(
            collective_id=0, has_side_effects=True, vmem_limit_bytes=64 * 1024 * 1024
        ),
    )(
        x_rows, expert_ids.reshape(1, rows), gates.reshape(1, rows), cotangent,
        w_gate, w_up, w_down,
    )
    igrad_shape = jax.ShapeDtypeStruct((rows, width), BF16)
    input_grad, gated_out, gate_grad, *weight_grads = pl.pallas_call(
        results_kernel,
        out_shape=(igrad_shape, *shapes),
        in_specs=[hbm] * 7,
        out_specs=[hbm] * 6,
        scratch_shapes=[
            *(pltpu.VMEM(shape.shape, shape.dtype) for shape in (back_shape, place_shape, igrad_shape, *shapes)),
            pltpu.SemaphoreType.DMA((7,)), pltpu.SemaphoreType.DMA((6,)),
        ],
        compiler_params=pltpu.CompilerParams(vmem_limit_bytes=64 * 1024 * 1024),
    )(back, place, gated, *others)
    return (gated_out, input_grad, gate_grad.reshape(rows, 1), *weight_grads)


def solution(mesh):
    in_specs = (
        P(("dp", "expert"), None),
        P(("dp", "expert"), None),
        P(("dp", "expert"), None),
        P(("dp", "expert"), None),
        P("expert", "dp", None),
        P("expert", "dp", None),
        P("expert", None, "dp"),
    )
    out_specs = (
        P(("dp", "expert"), None),
        P(("dp", "expert"), None),
        P(("dp", "expert"), None),
        P("expert", "dp", None),
        P("expert", "dp", None),
        P("expert", None, "dp"),
    )
    return jax.shard_map(
        per_device, mesh=mesh, in_specs=in_specs, out_specs=out_specs, check_vma=False
    )
```

```python
import functools

import jax
import jax.numpy as jnp
from jax import lax
from jax.experimental import pallas as pl
from jax.experimental.pallas import tpu as pltpu
from jax.sharding import PartitionSpec as P


def expert_rows(rows_in, rows_scaled, proj_gate, proj_up, proj_down):
    gate_act = jnp.dot(rows_in, proj_gate, preferred_element_type=jnp.float32)
    up_act = jnp.dot(rows_in, proj_up, preferred_element_type=jnp.float32)
    sigma = jax.nn.sigmoid(gate_act)
    hidden = (gate_act * sigma * up_act).astype(jnp.bfloat16)
    result = jnp.dot(hidden, proj_down, preferred_element_type=jnp.float32).astype(jnp.bfloat16)
    backed = jnp.dot(rows_scaled, proj_down.T, preferred_element_type=jnp.float32)
    d_gate_act = (backed * up_act * sigma * (1.0 + gate_act * (1.0 - sigma))).astype(jnp.bfloat16)
    d_up_act = (backed * gate_act * sigma).astype(jnp.bfloat16)
    d_input = (
        jnp.dot(d_gate_act, proj_gate.T, preferred_element_type=jnp.float32)
        + jnp.dot(d_up_act, proj_up.T, preferred_element_type=jnp.float32)
    ).astype(jnp.bfloat16)
    grad_g = jnp.dot(rows_in.T, d_gate_act, preferred_element_type=jnp.float32)
    grad_u = jnp.dot(rows_in.T, d_up_act, preferred_element_type=jnp.float32)
    grad_d = jnp.dot(hidden.T, rows_scaled, preferred_element_type=jnp.float32)
    return (result, d_input, (grad_g, grad_u, grad_d), (hidden, d_gate_act, d_up_act))


def rounded_sum(total, term):
    kept = lax.optimization_barrier(term.astype(jnp.bfloat16))
    return total + kept.astype(jnp.float32)


def collective_device(x_rows, expert_ids, gates, cotangent, w_gate, w_up, w_down):
    full_gate, full_up, full_down = (
        lax.all_gather(w_gate, "dp", axis=1, tiled=True),
        lax.all_gather(w_up, "dp", axis=1, tiled=True),
        lax.all_gather(w_down, "dp", axis=2, tiled=True),
    )
    proj_gate = full_gate[0]
    proj_up = full_up[0]
    proj_down = full_down[0]
    experts = lax.axis_size("expert")
    row_count = x_rows.shape[0]
    width = x_rows.shape[1]
    capacity = 2 * row_count // experts
    row_ids = expert_ids[:, 0]
    onehot = (row_ids[:, None] == jnp.arange(experts, dtype=jnp.int32)[None, :]).astype(jnp.int32)
    ranking = jnp.sum((jnp.cumsum(onehot, 0) - onehot) * onehot, 1)
    slot = row_ids * capacity + ranking
    counts = jnp.sum(onehot, 0)
    scaled = (gates * cotangent.astype(jnp.float32)).astype(jnp.bfloat16)
    send_in = (
        jnp.zeros((experts * capacity, width), jnp.bfloat16)
        .at[slot]
        .set(x_rows)
        .reshape(experts, capacity, width)
    )
    send_scaled = (
        jnp.zeros((experts * capacity, width), jnp.bfloat16)
        .at[slot]
        .set(scaled)
        .reshape(experts, capacity, width)
    )
    recv_in, recv_scaled, recv_counts = (
        lax.all_to_all(send_in, "expert", split_axis=0, concat_axis=0, tiled=True),
        lax.all_to_all(send_scaled, "expert", split_axis=0, concat_axis=0, tiled=True),
        lax.all_to_all(
            counts.reshape(experts, 1), "expert", split_axis=0, concat_axis=0, tiled=True
        ),
    )
    flat_in = recv_in.reshape(experts * capacity, width)
    flat_scaled = recv_scaled.reshape(experts * capacity, width)
    slot_out, slot_grad, grads, acts = expert_rows(
        flat_in, flat_scaled, proj_gate, proj_up, proj_down
    )
    back_result, back_input = (
        lax.all_to_all(
            slot_out.reshape(experts, capacity, width),
            "expert",
            split_axis=0,
            concat_axis=0,
            tiled=True,
        ),
        lax.all_to_all(
            slot_grad.reshape(experts, capacity, width),
            "expert",
            split_axis=0,
            concat_axis=0,
            tiled=True,
        ),
    )
    row_out = back_result.reshape(experts * capacity, width)[slot]
    input_grad = back_input.reshape(experts * capacity, width)[slot]
    gated_out = (gates * row_out.astype(jnp.float32)).astype(jnp.bfloat16)
    gate_grad = jnp.sum(
        cotangent.astype(jnp.float32) * row_out.astype(jnp.float32), 1, keepdims=True
    )
    groups = lax.axis_size("dp")
    rows_here = flat_in.shape[0]
    slice_in, slice_scaled = (
        lax.all_to_all(flat_in, "dp", split_axis=1, concat_axis=0, tiled=True),
        lax.all_to_all(flat_scaled, "dp", split_axis=1, concat_axis=0, tiled=True),
    )
    all_hidden, all_dgate, all_dup = (
        lax.all_gather(acts[0], "dp", axis=0, tiled=True),
        lax.all_gather(acts[1], "dp", axis=0, tiled=True),
        lax.all_gather(acts[2], "dp", axis=0, tiled=True),
    )
    quarter = slice_in.shape[1]
    hidden_units = all_hidden.shape[1]
    total_gate = jnp.zeros((quarter, hidden_units), jnp.float32)
    total_up = jnp.zeros((quarter, hidden_units), jnp.float32)
    total_down = jnp.zeros((hidden_units, quarter), jnp.float32)
    for group in range(groups):
        first_row = group * rows_here
        group_in = slice_in[first_row : first_row + rows_here]
        group_scaled = slice_scaled[first_row : first_row + rows_here]
        group_hidden = all_hidden[first_row : first_row + rows_here]
        group_dgate = all_dgate[first_row : first_row + rows_here]
        group_dup = all_dup[first_row : first_row + rows_here]
        total_gate = rounded_sum(
            total_gate, jnp.dot(group_in.T, group_dgate, preferred_element_type=jnp.float32)
        )
        total_up = rounded_sum(
            total_up, jnp.dot(group_in.T, group_dup, preferred_element_type=jnp.float32)
        )
        total_down = rounded_sum(
            total_down, jnp.dot(group_hidden.T, group_scaled, preferred_element_type=jnp.float32)
        )
    summed_gate = total_gate[None]
    summed_up = total_up[None]
    summed_down = total_down[None]
    return (
        gated_out,
        input_grad,
        gate_grad,
        summed_gate.astype(jnp.bfloat16),
        summed_up.astype(jnp.bfloat16),
        summed_down.astype(jnp.bfloat16),
    )


F32 = jnp.float32
BF16 = jnp.bfloat16


def dot(a, b):
    return lax.dot_general(a, b, (((1,), (0,)), ((), ())), preferred_element_type=F32)


def dot_left_t(a, b):
    return lax.dot_general(a, b, (((0,), (0,)), ((), ())), preferred_element_type=F32)


def dot_right_t(a, b):
    return lax.dot_general(a, b, (((1,), (1,)), ((), ())), preferred_element_type=F32)


def flipped(index, bits, size):
    result, place = 0, 1
    while place < size:
        digit = (index // place) % 2
        result = result + ((digit + 1) % 2 if bits & place else digit) * place
        place *= 2
    return result


def layer_kernel(
    n_dp, n_ex, cap,
    x_hbm, ids_hbm, gates_hbm, cot_hbm, wg_hbm, wu_hbm, wd_hbm,
    gated_hbm, in_back, ggrad_hbm, ogg_hbm, ogu_hbm, ogd_hbm, place_hbm,
    gated_ref, ggrad_ref, ogg_ref, ogu_ref, ogd_ref, row_place,
    x_ref, ids_ref, gates_ref, cot_ref,
    place_ref, send_x, send_s, recv_x, recv_s, out_send, in_send, out_back,
    full_g, full_u, full_d, hid_ref, fac_g, fac_u, dg_ref, du_ref, x_turned, hid_turned,
    part_g, part_u, part_d, got_g, got_u, got_d, sum_g, sum_u, sum_d,
    own_sem, out_sem, z_send, z_recv, w_send, w_recv, g_send, g_recv,
):
    me_e, me_d = lax.axis_index("expert"), lax.axis_index("dp")
    z_peers = [(k, flipped(me_e, k, n_ex)) for k in range(n_ex - 1, 0, -1)]
    side, over, across = (flipped(me_d, k, n_dp) for k in (1, 2, 3))
    rows, width = x_ref.shape
    piece = width // n_dp

    barrier = pltpu.get_barrier_semaphore()
    for _, peer in z_peers:
        pl.semaphore_signal(barrier, inc=1, device_id={"expert": peer}, device_id_type=pl.DeviceIdType.MESH)
    for peer in (side, over):
        pl.semaphore_signal(barrier, inc=1, device_id={"dp": peer}, device_id_type=pl.DeviceIdType.MESH)

    own = []
    for source, target in (
        (ids_hbm, ids_ref), (x_hbm, x_ref), (gates_hbm, gates_ref), (cot_hbm, cot_ref),
        (wg_hbm.at[0], full_g.at[me_d]), (wu_hbm.at[0], full_u.at[me_d]), (wd_hbm.at[0], full_d.at[me_d]),
    ):
        copy = pltpu.make_async_copy(source, target, own_sem.at[len(own)])
        copy.start()
        own.append(copy)

    def columns(q):
        return slice(q * piece, (q + 1) * piece)

    copies = []

    def remote(source, target, send_sem, recv_sem, axis, peer):
        copy = pltpu.make_async_remote_copy(
            src_ref=source,
            dst_ref=target,
            send_sem=send_sem,
            recv_sem=recv_sem,
            device_id={axis: peer},
            device_id_type=pl.DeviceIdType.MESH,
        )
        copy.start()
        copies.append(copy)
        return copy

    def slots(index):
        return pl.ds(pl.multiple_of(index * cap, cap), cap)

    def z_start(which, source, target, k):
        peer = flipped(me_e, k, n_ex)
        return remote(
            source.at[slots(peer)], target.at[slots(me_e)],
            z_send.at[which, k], z_recv.at[which, k], "expert", peer,
        )

    def z_own(source, target):
        target[slots(me_e), :] = source[slots(me_e), :]

    def w_start(which, source, target):
        return [
            remote(
                source.at[0], target.at[me_d],
                w_send.at[which, k], w_recv.at[which, k], "dp", peer,
            )
            for k, peer in enumerate((side, over))
        ]

    def w_pass(which, target, direct):
        half = target.shape[1] // 2
        first, second = target.at[side, pl.ds(0, half)], target.at[over, pl.ds(half, half)]
        direct[0].wait_recv()
        one = remote(first, first, w_send.at[which, 2], w_recv.at[which, 2], "dp", over)
        direct[1].wait_recv()
        two = remote(second, second, w_send.at[which, 3], w_recv.at[which, 3], "dp", side)
        return [one, two]

    def g_start(which, part, got):
        half = part.shape[1] // 2
        upper, lower = pl.ds(0, half), pl.ds(half, half)
        made = {}
        for slot, source, peer in (
            (1, part.at[across, upper], side),
            (3, part.at[across, lower], over),
            (0, part.at[side, upper], side),
            (2, part.at[over, lower], over),
        ):
            made[slot] = remote(
                source, got.at[slot], g_send.at[which, slot], g_recv.at[which, slot], "dp", peer
            )
        return made

    def g_pass(which, part, got, total, made):
        half = part.shape[1] // 2
        for slot, peer, rows_of in ((1, over, pl.ds(0, half)), (3, side, pl.ds(half, half))):
            made[slot].wait_recv()
            index, later = slot // 2, 4 + slot // 2
            total[index] = (part[peer, rows_of].astype(F32) + got[slot].astype(F32)).astype(BF16)
            made[later] = remote(
                total.at[index], got.at[later], g_send.at[which, later], g_recv.at[which, later], "dp", peer
            )

    def g_finish(part, got, made, out):
        half = part.shape[1] // 2
        for slot, later, rows_of in ((0, 4, pl.ds(0, half)), (2, 5, pl.ds(half, half))):
            made[slot].wait_recv()
            made[later].wait_recv()
            out[0, rows_of] = (
                part[me_d, rows_of].astype(F32) + got[slot].astype(F32) + got[later].astype(F32)
            ).astype(BF16)

    stored = []

    def store(source, target):
        copy = pltpu.make_async_copy(source, target, out_sem.at[len(stored)])
        copy.start()
        stored.append(copy)

    def arrived(made):
        for copy in made:
            copy.wait_recv()

    far = [k for k in range(n_ex - 1, 0, -1) if k >= n_ex // 2]
    near = [k for k in range(n_ex - 1, 0, -1) if k < n_ex // 2]

    own[0].wait()
    ids = ids_ref[...]
    onehot = (ids == lax.broadcasted_iota(jnp.int32, (n_ex, rows), 0)).astype(F32)
    row_a = lax.broadcasted_iota(jnp.int32, (rows, rows), 0)
    row_b = lax.broadcasted_iota(jnp.int32, (rows, rows), 1)
    ranks = jnp.sum(dot(onehot.astype(BF16), (row_a < row_b).astype(BF16)) * onehot, 0, keepdims=True)
    slot = ids * cap + ranks.astype(jnp.int32)
    place_ref[...] = (slot == lax.broadcasted_iota(jnp.int32, (n_ex * cap, rows), 0)).astype(BF16)
    own[1].wait()
    send_x[...] = dot(place_ref[...], x_ref[...]).astype(BF16)

    pl.semaphore_wait(barrier, n_ex + 1)

    x_far = [z_start(0, send_x, recv_x, k) for k in far]
    g_direct = w_start(0, wg_hbm, full_g)
    u_direct = w_start(1, wu_hbm, full_u)
    x_near = [z_start(0, send_x, recv_x, k) for k in near]

    own[2].wait()
    own[3].wait()
    diagonal = row_a == row_b
    gates = jnp.sum(jnp.where(diagonal, gates_ref[...], 0.0), 1, keepdims=True)
    scaled = (gates * cot_ref[...].astype(F32)).astype(BF16)
    send_s[...] = dot(place_ref[...], scaled).astype(BF16)
    s_copies = [z_start(1, send_s, recv_s, k) for k in near]
    slot_of_row = jnp.sum(jnp.where(diagonal, slot, 0), 1, keepdims=True)
    row_place[...] = (slot_of_row == lax.broadcasted_iota(jnp.int32, (rows, n_ex * cap), 1)).astype(BF16)
    z_own(send_x, recv_x)
    z_own(send_s, recv_s)
    store(row_place, place_hbm)

    g_passed = w_pass(0, full_g, g_direct)
    d_direct = w_start(2, wd_hbm, full_d)
    s_copies += [z_start(1, send_s, recv_s, k) for k in far]
    u_passed = w_pass(1, full_u, u_direct)
    hidden_units = wg_hbm.shape[2]
    arrived(x_far + x_near)
    arrived(g_passed)
    own[4].wait()
    gate_act = dot(recv_x[...], full_g[...].reshape(width, hidden_units))
    d_passed = w_pass(2, full_d, d_direct)
    arrived(u_passed)
    own[5].wait()
    up_act = dot(recv_x[...], full_u[...].reshape(width, hidden_units))
    sigma = jax.nn.sigmoid(gate_act)
    hid_ref[...] = (gate_act * sigma * up_act).astype(BF16)
    fac_g[...] = up_act * sigma * (1.0 + gate_act * (1.0 - sigma))
    fac_u[...] = gate_act * sigma
    arrived(d_passed)
    own[6].wait()
    for q in range(n_dp):
        out_send[:, columns(q)] = dot(hid_ref[...], full_d[q]).astype(BF16)
    out_copies = [z_start(2, out_send, out_back, k) for k in far + near]
    z_own(out_send, out_back)
    x_turned[...] = recv_x[...].T
    hid_turned[...] = hid_ref[...].T

    arrived(s_copies)
    for q in range(n_dp):
        part_d[q] = dot(hid_turned[...], recv_s[:, columns(q)]).astype(BF16)
    pd_copies = g_start(2, part_d, got_d)
    backed = dot_right_t(recv_s[:, columns(0)], full_d[0])
    for q in range(1, n_dp):
        backed = backed + dot_right_t(recv_s[:, columns(q)], full_d[q])
    dg_ref[...] = (backed * fac_g[...]).astype(BF16)
    du_ref[...] = (backed * fac_u[...]).astype(BF16)
    for q in range(n_dp):
        part_g[q] = dot(x_turned[columns(q), :], dg_ref[...]).astype(BF16)
    pg_copies = g_start(0, part_g, got_g)
    for q in range(n_dp):
        part_u[q] = dot(x_turned[columns(q), :], du_ref[...]).astype(BF16)
    pu_copies = g_start(1, part_u, got_u)
    for q in range(n_dp):
        in_send[:, columns(q)] = (
            dot_right_t(dg_ref[...], full_g[q]) + dot_right_t(du_ref[...], full_u[q])
        ).astype(BF16)
    in_copies = [z_start(3, in_send, in_back, k) for k in far + near]
    store(in_send.at[slots(me_e)], in_back.at[slots(me_e)])
    g_pass(2, part_d, got_d, sum_d, pd_copies)
    g_pass(0, part_g, got_g, sum_g, pg_copies)
    g_pass(1, part_u, got_u, sum_u, pu_copies)

    arrived(out_copies)
    row_out = dot(row_place[...], out_back[...])
    gated_ref[...] = (gates * row_out).astype(BF16)
    row_sums = jnp.sum(cot_ref[...].astype(F32) * row_out, 1, keepdims=True)
    ggrad_ref[...] = jnp.sum(jnp.where(diagonal, row_sums, 0.0), 0, keepdims=True)
    store(gated_ref, gated_hbm)
    store(ggrad_ref, ggrad_hbm)
    g_finish(part_d, got_d, pd_copies, ogd_ref)
    store(ogd_ref, ogd_hbm)
    g_finish(part_g, got_g, pg_copies, ogg_ref)
    store(ogg_ref, ogg_hbm)
    g_finish(part_u, got_u, pu_copies, ogu_ref)
    store(ogu_ref, ogu_hbm)
    arrived(in_copies)
    for copy in copies:
        copy.wait_send()
    for copy in stored:
        copy.wait()


def results_kernel(*refs):
    back_hbm, place_hbm, *sources = refs[:7]
    igrad_hbm, *targets = refs[7:13]
    back, place, igrad, *held = refs[13:21]
    in_sem, out_sem = refs[21:]
    first = [
        pltpu.make_async_copy(back_hbm, back, in_sem.at[5]),
        pltpu.make_async_copy(place_hbm, place, in_sem.at[6]),
    ]
    reads = [pltpu.make_async_copy(sources[i], held[i], in_sem.at[i]) for i in range(5)]
    writes = [pltpu.make_async_copy(held[i], targets[i], out_sem.at[i]) for i in range(5)]
    for read in first + reads:
        read.start()
    for read in first:
        read.wait()
    igrad[...] = dot(place[...], back[...]).astype(BF16)
    last = pltpu.make_async_copy(igrad, igrad_hbm, out_sem.at[5])
    last.start()
    for read, write in zip(reads, writes):
        read.wait()
        write.start()
    for write in writes + [last]:
        write.wait()


def power_of_two(size):
    return size & (size - 1) == 0


def per_device(x_rows, expert_ids, gates, cotangent, w_gate, w_up, w_down):
    n_dp, n_ex = lax.axis_size("dp"), lax.axis_size("expert")
    rows, width = x_rows.shape
    cap = 2 * rows // n_ex
    _, piece, hidden = w_gate.shape
    if cap % 16 or piece % 32 or hidden % 32 or not power_of_two(n_ex) or n_ex < 4 or n_dp != 4:
        return collective_device(x_rows, expert_ids, gates, cotangent, w_gate, w_up, w_down)
    total = n_ex * cap
    hbm = pl.BlockSpec(memory_space=pltpu.HBM)
    slots_of = pltpu.VMEM((total, width), BF16)
    gates_of = pltpu.VMEM((n_dp, piece, hidden), BF16)
    downs_of = pltpu.VMEM((n_dp, hidden, piece), BF16)
    got_gates = pltpu.VMEM((6, piece // 2, hidden), BF16)
    got_downs = pltpu.VMEM((6, hidden // 2, piece), BF16)
    sum_gates = pltpu.VMEM((2, piece // 2, hidden), BF16)
    sum_downs = pltpu.VMEM((2, hidden // 2, piece), BF16)
    acts_of = pltpu.VMEM((total, hidden), BF16)
    facs_of = pltpu.VMEM((total, hidden), F32)
    shapes = (
        jax.ShapeDtypeStruct((rows, width), BF16),
        jax.ShapeDtypeStruct((1, rows), F32),
        jax.ShapeDtypeStruct(w_gate.shape, BF16),
        jax.ShapeDtypeStruct(w_up.shape, BF16),
        jax.ShapeDtypeStruct(w_down.shape, BF16),
    )
    back_shape = jax.ShapeDtypeStruct((total, width), BF16)
    place_shape = jax.ShapeDtypeStruct((rows, total), BF16)
    gated, back, *others, place = pl.pallas_call(
        functools.partial(layer_kernel, n_dp, n_ex, cap),
        out_shape=(shapes[0], back_shape, *shapes[1:], place_shape),
        in_specs=[hbm] * 7,
        out_specs=[hbm] * 7,
        scratch_shapes=[
            *(pltpu.VMEM(shape.shape, shape.dtype) for shape in (*shapes, place_shape)),
            pltpu.VMEM((rows, width), BF16), pltpu.VMEM((1, rows), jnp.int32),
            pltpu.VMEM((1, rows), F32), pltpu.VMEM((rows, width), BF16),
            pltpu.VMEM((total, rows), BF16),
            slots_of, slots_of, slots_of, slots_of, slots_of, slots_of, slots_of,
            gates_of, gates_of, downs_of,
            acts_of, facs_of, facs_of, acts_of, acts_of,
            pltpu.VMEM((width, total), BF16), pltpu.VMEM((hidden, total), BF16),
            gates_of, gates_of, downs_of,
            got_gates, got_gates, got_downs, sum_gates, sum_gates, sum_downs,
            pltpu.SemaphoreType.DMA((7,)), pltpu.SemaphoreType.DMA((7,)),
            pltpu.SemaphoreType.DMA((4, n_ex)), pltpu.SemaphoreType.DMA((4, n_ex)),
            pltpu.SemaphoreType.DMA((3, 4)), pltpu.SemaphoreType.DMA((3, 4)),
            pltpu.SemaphoreType.DMA((3, 6)), pltpu.SemaphoreType.DMA((3, 6)),
        ],
        compiler_params=pltpu.CompilerParams(
            collective_id=0, has_side_effects=True, vmem_limit_bytes=64 * 1024 * 1024
        ),
    )(
        x_rows, expert_ids.reshape(1, rows), gates.reshape(1, rows), cotangent,
        w_gate, w_up, w_down,
    )
    igrad_shape = jax.ShapeDtypeStruct((rows, width), BF16)
    input_grad, gated_out, gate_grad, *weight_grads = pl.pallas_call(
        results_kernel,
        out_shape=(igrad_shape, *shapes),
        in_specs=[hbm] * 7,
        out_specs=[hbm] * 6,
        scratch_shapes=[
            *(pltpu.VMEM(shape.shape, shape.dtype) for shape in (back_shape, place_shape, igrad_shape, *shapes)),
            pltpu.SemaphoreType.DMA((7,)), pltpu.SemaphoreType.DMA((6,)),
        ],
        compiler_params=pltpu.CompilerParams(vmem_limit_bytes=64 * 1024 * 1024),
    )(back, place, gated, *others)
    return (gated_out, input_grad, gate_grad.reshape(rows, 1), *weight_grads)


def solution(mesh):
    in_specs = (
        P(("dp", "expert"), None),
        P(("dp", "expert"), None),
        P(("dp", "expert"), None),
        P(("dp", "expert"), None),
        P("expert", "dp", None),
        P("expert", "dp", None),
        P("expert", None, "dp"),
    )
    out_specs = (
        P(("dp", "expert"), None),
        P(("dp", "expert"), None),
        P(("dp", "expert"), None),
        P("expert", "dp", None),
        P("expert", "dp", None),
        P("expert", None, "dp"),
    )
    return jax.shard_map(
        per_device, mesh=mesh, in_specs=in_specs, out_specs=out_specs, check_vma=False
    )
```
